1024 devices in a mesh: ctx: 64 (over x, z), exp: 16 (over y, core).
Axes of the slice: x: 8, y: 8, z: 8, core: 2. Of those that a mesh axis runs over, the one named last changes fastest.
Arguments:
- layer_input: bfloat16 [16, 8192, 3072], P('exp', 'ctx'), may hold values from -6 to 6
- expert_ids: int32 [16, 8192, 2], P('exp', 'ctx'), may hold values from 0 to 15, as said below
- router_probs: float32 [16, 8192, 16], P('exp', 'ctx'), may hold values from 0 to 1, as said below
- router_weight: bfloat16 [16, 3072], replicated, may hold values from -1.5 to 1.5
- expert_grads: bfloat16 [64, 16, 320, 3072], P('ctx', 'exp'), may hold values from -6 to 6
- gate_dots: bfloat16 [64, 16, 320], P('ctx', 'exp'), may hold values from -12 to 12
Outputs:
- moe_input_grad: bfloat16 [16, 8192, 3072], P('exp', 'ctx')
- router_weight_grad: float32 [16, 3072], P('exp')
The draws below stay inside these ranges and needn't reach their ends.
Inputs may be any that keep to these rules, and one draw needn't show every extreme that they name: `expert_ids`: in each aligned block of 128 rows of a window (the rows of one device) every expert is named at least once and at most 20 times, and some expert exactly 20 times; a row names 2 different experts. `router_probs`: each row is positive and sums to one; the experts that expert_ids names in a row hold that row's largest probabilities.
All inputs are finite; a program needn't handle non-finite values.
Results may differ from the reference program's by a relative error of at most 0.0033.
Values may be sent and summed in bfloat16 or wider, within the bound.
No kernel may reach another device: no remote copies, remote signals or barrier semaphores. Data moves between devices by JAX's collectives and lax.ppermute only.
A program may use at most 32 MiB of HBM per device.

```python
import jax
import jax.numpy as jnp
from jax import lax

D = 3072
EXPERTS = 16
TOP = 2
TOK_DEV = 128
LENGTH = 8192
CAP = 20
N_CTX = 64
N_EXP = 16


def route_plan(key):
    perm_key, count_key, order_key = jax.random.split(key, 3)
    block_count = N_EXP * N_CTX
    pool_size = EXPERTS // TOP
    expert_order = jax.vmap(lambda one_key: jax.random.permutation(one_key, EXPERTS))(jax.random.split(perm_key, block_count)).astype(jnp.int32)
    remaining = jnp.full((block_count, TOP), TOK_DEV - CAP, jnp.int32)
    count_list = [jnp.full((block_count, TOP), CAP, jnp.int32)]
    for slot_pos in range(1, pool_size - 1):
        later = pool_size - 1 - slot_pos
        lower = jnp.maximum(1, remaining - later * CAP)
        upper = jnp.minimum(CAP, remaining - later)
        drawn = jax.random.randint(jax.random.fold_in(count_key, slot_pos), (block_count, TOP), lower, upper + 1).astype(jnp.int32)
        count_list.append(drawn)
        remaining = remaining - drawn
    if pool_size > 1:
        count_list.append(remaining)
    counts = jnp.stack(count_list, axis=-1)
    bounds = jnp.cumsum(counts, axis=-1)
    row_order = jax.vmap(lambda one_key: jax.random.permutation(one_key, TOK_DEV))(jax.random.split(order_key, block_count * TOP)).astype(jnp.int32)
    row_rank = row_order.reshape(block_count, TOP, TOK_DEV)
    bucket = jnp.sum((row_rank[..., None] >= bounds[:, :, None, :]).astype(jnp.int32), axis=-1)
    column_base = (jnp.arange(TOP, dtype=jnp.int32) * pool_size)[None, :, None]
    position = (column_base + bucket).reshape(block_count, TOP * TOK_DEV)
    chosen = jnp.take_along_axis(expert_order, position, axis=1).reshape(block_count, TOP, TOK_DEV)
    return jnp.transpose(chosen, (0, 2, 1)).reshape(N_EXP, LENGTH, TOP).astype(jnp.int32)


def draw_expert_ids(key, part):
    return route_plan(key)


def draw_router_probs(key, part):
    chosen_ids = route_plan(key)
    key = jax.random.fold_in(key, 7)
    high_key, low_key = jax.random.split(key)
    chosen_mask = jnp.any(chosen_ids[..., None] == jnp.arange(EXPERTS, dtype=jnp.int32), axis=2)
    high_draw = jax.random.uniform(high_key, (N_EXP, LENGTH, EXPERTS), jnp.float32)
    low_draw = jax.random.uniform(low_key, (N_EXP, LENGTH, EXPERTS), jnp.float32)
    logits = jnp.where(chosen_mask, 0.2 + 3.5 * high_draw, -4.0 * low_draw)
    weights = jnp.exp(logits)
    return weights / jnp.sum(weights, axis=-1, keepdims=True)


def block_levels(stream_key, shape, pieces, smallest, largest):
    loudness, own = 1.0, jax.random.fold_in(stream_key, 6)
    for dim, parts in pieces:
        draws = jnp.exp(jax.random.uniform(jax.random.fold_in(own, dim), (parts,), jnp.float32, smallest / len(pieces), largest / len(pieces)))
        loudness = loudness * jnp.repeat(draws, shape[dim] // parts).reshape([-1 if axis == dim else 1 for axis in range(len(shape))])
    return loudness


def normal_values(own_key, shape, scale, limit, cuts=(), held_as=jnp.bfloat16):
    array = jax.random.normal(own_key, shape, jnp.float32) * scale
    if len(cuts) > 0:
        array = block_levels(own_key, shape, cuts, -0.22, 0.18) * array
    return jnp.clip(array, min=-limit, max=limit).astype(held_as)


def setup_inputs(seed: int = 0) -> dict:
    seeds = jax.random.split(jax.random.key(seed), 7)
    return {
        "layer_input": normal_values(seeds[0], (N_EXP, LENGTH, D), 1.0, 6.0, ((0, 16), (1, 64))),
        "expert_ids": draw_expert_ids(jax.random.fold_in(seeds[6], 71), 0),
        "router_probs": draw_router_probs(jax.random.fold_in(seeds[6], 71), 0),
        "router_weight": normal_values(seeds[3], (EXPERTS, D), EXPERTS ** -0.5, 1.5),
        "expert_grads": normal_values(seeds[4], (N_CTX, EXPERTS, N_EXP * CAP, D), 1.0, 6.0, ((0, 64), (1, 16))),
        "gate_dots": normal_values(seeds[5], (N_CTX, EXPERTS, N_EXP * CAP), 2.0, 12.0, ((0, 64), (1, 16))),
    }


def combine_window(window, choice_ids, prob_rows, input_rows, router_weight, expert_grads, gate_dots):
    grad_slab = lax.dynamic_slice_in_dim(expert_grads, (window * CAP).astype(jnp.int32), CAP, 2)
    dot_slab = lax.dynamic_slice_in_dim(gate_dots, (window * CAP).astype(jnp.int32), CAP, 2)
    copy_table = grad_slab.reshape(N_CTX, EXPERTS * CAP, D)
    dot_table = dot_slab.reshape(N_CTX, EXPERTS * CAP).astype(jnp.float32)
    flat_choice = choice_ids.reshape(N_CTX, TOK_DEV * TOP)
    onehot = (flat_choice[..., None] == jnp.arange(EXPERTS, dtype=jnp.int32)).astype(jnp.int32)
    prior_count = jnp.cumsum(onehot, axis=1) - onehot
    slot_number = jnp.sum(prior_count * onehot, axis=-1)
    slot_index = (flat_choice * CAP + slot_number).astype(jnp.int32)
    copy_rows = jnp.take_along_axis(copy_table, slot_index[..., None], axis=1).astype(jnp.float32).reshape(LENGTH, TOP, D)
    gate_grad = jnp.take_along_axis(dot_table, slot_index, axis=1).reshape(LENGTH, TOP)
    choice_mask = (choice_ids[..., None] == jnp.arange(EXPERTS, dtype=jnp.int32)).astype(jnp.float32)
    picked = jnp.sum(choice_mask * prob_rows[:, None, :], axis=-1)
    exp_total = jnp.sum(picked, axis=1, keepdims=True)
    gate_value = picked / exp_total
    pick_grad = gate_grad / exp_total - jnp.sum(gate_grad * picked, axis=1, keepdims=True) / (exp_total * exp_total)
    router_grad = jnp.sum(choice_mask * pick_grad[..., None], axis=1)
    logit_grad = (prob_rows * (router_grad - jnp.sum(prob_rows * router_grad, axis=1, keepdims=True))).astype(jnp.bfloat16)
    router_term = jnp.dot(logit_grad, router_weight, preferred_element_type=jnp.float32)
    combined = jnp.sum(gate_value[..., None] * copy_rows, axis=1) + router_term
    weight_term = jnp.dot(logit_grad.T, input_rows, preferred_element_type=jnp.float32)
    return combined.astype(jnp.bfloat16), weight_term


def reference(layer_input, expert_ids, router_probs, router_weight, expert_grads, gate_dots):
    def combine_one(window):
        return combine_window(window, expert_ids[window], router_probs[window], layer_input[window], router_weight, expert_grads, gate_dots)

    moe_input_grad, weight_terms = lax.map(combine_one, jnp.arange(N_EXP, dtype=jnp.int32))
    router_weight_grad = jnp.sum(weight_terms, axis=0)
    return (moe_input_grad, router_weight_grad)
```

```python
import jax
import jax.numpy as jnp
from jax import lax
from jax.experimental import pallas as pl
from jax.experimental.pallas import tpu as pltpu
from jax.sharding import PartitionSpec as P

QUARTERS = 4
LANES = 128
VMEM = 48 * 1024 * 1024


def dot_rows(left, right):
    return lax.dot_general(
        left, right, (((0,), (0,)), ((), ())), preferred_element_type=jnp.float32
    )


def gate_pack_kernel(cap, dots_ref, out_ref):
    windows, lanes = out_ref.shape[0], out_ref.shape[2]
    count = dots_ref.shape[1]
    column = lax.broadcasted_iota(jnp.int32, (windows, count), 1)
    first = lax.broadcasted_iota(jnp.int32, (windows, count), 0) * cap
    dots = jnp.broadcast_to(dots_ref[...].astype(jnp.float32), (windows, count))
    own = jnp.where((column >= first) & (column < first + cap), dots, 0.0)
    slot = lax.broadcasted_iota(jnp.int32, (count, lanes), 0) % cap
    lane = lax.broadcasted_iota(jnp.int32, (count, lanes), 1)
    place = jnp.where(slot == lane, 1.0, 0.0)
    laid = jnp.dot(
        own.astype(jnp.bfloat16), place.astype(jnp.bfloat16), preferred_element_type=jnp.float32
    )
    out_ref[...] = laid[:, None, :]


def pack_kernel(cap, rows_ref, out_ref):
    part = out_ref.shape[2]
    rows = rows_ref[...].astype(jnp.float32)
    for w in range(out_ref.shape[0]):
        window = rows[w * cap : (w + 1) * cap]
        stacked = jnp.concatenate(
            [window[:, q * part : (q + 1) * part] for q in range(QUARTERS)], axis=0
        )
        out_ref[w] = stacked.astype(jnp.bfloat16)


def router_kernel(ids_ref, probs_ref, dots_ref, input_ref, logit_ref, place_ref, term_ref):
    experts, tokens = probs_ref.shape
    probs = probs_ref[...]
    expert = lax.broadcasted_iota(jnp.int32, (experts, tokens), 0)
    chosen = [expert == ids_ref[k : k + 1, :] for k in range(2)]
    mask = jnp.where(chosen[0] | chosen[1], 1.0, 0.0)
    earlier = lax.broadcasted_iota(jnp.int32, (tokens, tokens), 0) < lax.broadcasted_iota(
        jnp.int32, (tokens, tokens), 1
    )
    prior = jnp.dot(
        mask.astype(jnp.bfloat16),
        jnp.where(earlier, 1.0, 0.0).astype(jnp.bfloat16),
        preferred_element_type=jnp.float32,
    )
    dots = dots_ref[...][:, 0, :].astype(jnp.bfloat16)
    lane_count = dots.shape[1]
    slot_row = lax.broadcasted_iota(jnp.int32, (lane_count, tokens), 0)
    picked, gate_grad, slots = [], [], []
    for k in range(2):
        onehot = jnp.where(chosen[k], 1.0, 0.0)
        picked.append(jnp.sum(jnp.where(chosen[k], probs, 0.0), axis=0, keepdims=True))
        slot = jnp.sum(onehot * prior, axis=0, keepdims=True).astype(jnp.int32)
        slots.append(slot)
        values = dot_rows(dots, onehot.astype(jnp.bfloat16))
        gate_grad.append(jnp.sum(jnp.where(slot_row == slot, values, 0.0), axis=0, keepdims=True))
    total = picked[0] + picked[1]
    shared = (gate_grad[0] * picked[0] + gate_grad[1] * picked[1]) / (total * total)
    router_grad = sum(
        jnp.where(chosen[k], gate_grad[k] / total - shared, 0.0) for k in range(2)
    )
    logit = probs * (router_grad - jnp.sum(probs * router_grad, axis=0, keepdims=True))
    logit = logit.astype(jnp.bfloat16)
    logit_ref[...] = logit
    place_ref[...] = jnp.concatenate(
        [picked[0] / total, picked[1] / total]
        + [s.astype(jnp.float32) for s in slots]
        + [jnp.zeros((4, tokens), jnp.float32)],
        axis=0,
    )
    term = jnp.dot(logit, input_ref[...], preferred_element_type=jnp.float32)
    term_ref[...] = term[:, None, :]


def combine_kernel(cap, ids_ref, place_ref, logit_ref, weight_ref, copies_ref, out_ref):
    experts, depth, part = copies_ref.shape
    tokens = ids_ref.shape[1]
    copies = copies_ref[...].reshape(experts * depth, part)
    row = lax.broadcasted_iota(jnp.int32, (experts * depth, tokens), 0)
    gates = [place_ref[k : k + 1, :] for k in range(2)]
    base = [
        ids_ref[k : k + 1, :] * depth + place_ref[2 + k : 3 + k, :].astype(jnp.int32)
        for k in range(2)
    ]
    for q in range(QUARTERS):
        spread = jnp.where(row == base[0] + q * cap, gates[0], 0.0) + jnp.where(
            row == base[1] + q * cap, gates[1], 0.0
        )
        high = spread.astype(jnp.bfloat16)
        low = (spread - high.astype(jnp.float32)).astype(jnp.bfloat16)
        columns = slice(q * part, (q + 1) * part)
        total = dot_rows(high, copies) + dot_rows(low, copies)
        total = total + dot_rows(logit_ref[...], weight_ref[:, columns])
        out_ref[:, columns] = total.astype(jnp.bfloat16)


def shards(side, layer_input, expert_ids, router_probs, router_weight, expert_grads, gate_dots):
    slots, width = expert_grads.shape[2:]
    tokens, experts = router_probs.shape[1:]
    windows = lax.axis_size("exp")
    cap = slots // windows
    part = width // QUARTERS
    depth = cap * QUARTERS
    params = pltpu.CompilerParams(vmem_limit_bytes=VMEM)

    laid = pl.pallas_call(
        lambda *refs: gate_pack_kernel(cap, *refs),
        out_shape=jax.ShapeDtypeStruct((windows, 1, LANES), jnp.float32),
        compiler_params=params,
    )(gate_dots[0])
    dots = lax.all_to_all(laid, "exp", 0, 0, tiled=True)

    packed = pl.pallas_call(
        lambda *refs: pack_kernel(cap, *refs),
        out_shape=jax.ShapeDtypeStruct((windows, depth, part), jnp.bfloat16),
        grid=(windows // 4,),
        in_specs=[pl.BlockSpec((4 * cap, width), lambda g: (g, 0))],
        out_specs=pl.BlockSpec((4, depth, part), lambda g: (g, 0, 0)),
        compiler_params=params,
    )(expert_grads[0, 0])
    copies = lax.all_to_all(packed, "exp", 0, 0, tiled=True)

    ids = jnp.swapaxes(expert_ids, 1, 2)[0]
    probs = jnp.swapaxes(router_probs, 1, 2)[0]
    logit, place, term = pl.pallas_call(
        router_kernel,
        out_shape=(
            jax.ShapeDtypeStruct((experts, tokens), jnp.bfloat16),
            jax.ShapeDtypeStruct((8, tokens), jnp.float32),
            jax.ShapeDtypeStruct((experts, 1, width), jnp.float32),
        ),
        compiler_params=params,
    )(ids, probs, dots, layer_input[0])

    own = jnp.sum(lax.all_to_all(term, "exp", 0, 0, tiled=True), axis=0)
    across = [[x * side + z for x in range(side)] for z in range(side)]
    along = [[x * side + z for z in range(side)] for x in range(side)]
    for groups in (across, along):
        copied = jnp.broadcast_to(own[None], (side,) + own.shape)
        own = jnp.sum(
            lax.all_to_all(copied, "ctx", 0, 0, axis_index_groups=groups, tiled=True), axis=0
        )

    combined = pl.pallas_call(
        lambda *refs: combine_kernel(cap, *refs),
        out_shape=jax.ShapeDtypeStruct((tokens, width), jnp.bfloat16),
        compiler_params=params,
    )(ids, place, logit, router_weight, copies)
    return combined[None], own


def solution(mesh):
    in_specs = (
        P("exp", "ctx", None),
        P("exp", "ctx", None),
        P("exp", "ctx", None),
        P(),
        P("ctx", "exp", None, None),
        P("ctx", "exp", None),
    )
    out_specs = (P("exp", "ctx", None), P("exp", None))
    side = round(mesh.shape["ctx"] ** 0.5)

    def step(*arrays):
        return shards(side, *arrays)

    return jax.shard_map(step, mesh=mesh, in_specs=in_specs, out_specs=out_specs, check_vma=False)
```

```python
import jax
import jax.numpy as jnp
from jax import lax
from jax.experimental import pallas as pl
from jax.experimental.pallas import tpu as pltpu
from jax.sharding import PartitionSpec as P

QUARTERS = 4
STEPS = (0, 3, 5, 2, 6, 4, 1, 7)
LANES = 128
VMEM = 48 * 1024 * 1024


def dot_rows(left, right):
    return lax.dot_general(
        left, right, (((0,), (0,)), ((), ())), preferred_element_type=jnp.float32
    )


def gate_pack_kernel(cap, dots_ref, out_ref):
    windows, lanes = out_ref.shape[0], out_ref.shape[2]
    count = dots_ref.shape[1]
    column = lax.broadcasted_iota(jnp.int32, (windows, count), 1)
    first = lax.broadcasted_iota(jnp.int32, (windows, count), 0) * cap
    dots = jnp.broadcast_to(dots_ref[...].astype(jnp.float32), (windows, count))
    own = jnp.where((column >= first) & (column < first + cap), dots, 0.0)
    slot = lax.broadcasted_iota(jnp.int32, (count, lanes), 0) % cap
    lane = lax.broadcasted_iota(jnp.int32, (count, lanes), 1)
    place = jnp.where(slot == lane, 1.0, 0.0)
    laid = jnp.dot(
        own.astype(jnp.bfloat16), place.astype(jnp.bfloat16), preferred_element_type=jnp.float32
    )
    out_ref[...] = laid[:, None, :]


def pack_kernel(cap, rows_ref, kept_ref, given_ref):
    part = kept_ref.shape[2]
    core = lax.axis_index("exp") % 2
    rows = rows_ref[...].astype(jnp.float32)
    for pair in range(kept_ref.shape[0]):
        stacks = []
        for w in (2 * pair, 2 * pair + 1):
            window = rows[w * cap : (w + 1) * cap]
            stacked = jnp.concatenate(
                [window[:, q * part : (q + 1) * part] for q in range(QUARTERS)], axis=0
            )
            stacks.append(stacked)
        kept_ref[pair] = jnp.where(core == 0, stacks[0], stacks[1]).astype(jnp.bfloat16)
        given_ref[pair] = jnp.where(core == 0, stacks[1], stacks[0]).astype(jnp.bfloat16)


def deal_kernel(kept_ref, got_ref, *out_refs):
    chips = kept_ref.shape[0]
    chip = lax.axis_index("exp") // 2
    for step, out_ref in zip(STEPS, out_refs):
        target = (chip + step) % chips
        out_ref[0] = kept_ref[target]
        out_ref[1] = got_ref[target]


def router_kernel(depth, ids_ref, probs_ref, dots_ref, input_ref, logit_ref, place_ref, term_ref):
    experts, tokens = probs_ref.shape
    probs = probs_ref[...]
    expert = lax.broadcasted_iota(jnp.int32, (experts, tokens), 0)
    chosen = [expert == ids_ref[k : k + 1, :] for k in range(2)]
    mask = jnp.where(chosen[0] | chosen[1], 1.0, 0.0)
    earlier = lax.broadcasted_iota(jnp.int32, (tokens, tokens), 0) < lax.broadcasted_iota(
        jnp.int32, (tokens, tokens), 1
    )
    prior = jnp.dot(
        mask.astype(jnp.bfloat16),
        jnp.where(earlier, 1.0, 0.0).astype(jnp.bfloat16),
        preferred_element_type=jnp.float32,
    )
    dots = dots_ref[...][:, 0, :].astype(jnp.bfloat16)
    lane_count = dots.shape[1]
    slot_row = lax.broadcasted_iota(jnp.int32, (lane_count, tokens), 0)
    picked, gate_grad, slots = [], [], []
    for k in range(2):
        onehot = jnp.where(chosen[k], 1.0, 0.0)
        picked.append(jnp.sum(jnp.where(chosen[k], probs, 0.0), axis=0, keepdims=True))
        slot = jnp.sum(onehot * prior, axis=0, keepdims=True).astype(jnp.int32)
        slots.append(slot)
        values = dot_rows(dots, onehot.astype(jnp.bfloat16))
        gate_grad.append(jnp.sum(jnp.where(slot_row == slot, values, 0.0), axis=0, keepdims=True))
    total = picked[0] + picked[1]
    shared = (gate_grad[0] * picked[0] + gate_grad[1] * picked[1]) / (total * total)
    router_grad = sum(
        jnp.where(chosen[k], gate_grad[k] / total - shared, 0.0) for k in range(2)
    )
    logit = probs * (router_grad - jnp.sum(probs * router_grad, axis=0, keepdims=True))
    logit = logit.astype(jnp.bfloat16)
    logit_ref[...] = logit
    chip, core = lax.axis_index("exp") // 2, lax.axis_index("exp") % 2
    rows = []
    for k in range(2):
        ids = ids_ref[k : k + 1, :]
        step = (chip - ids // 2 + experts // 2) % (experts // 2)
        place = sum(jnp.where(step == STEPS[n], n, 0) for n in range(len(STEPS)))
        block = place * 2 + (ids % 2 + core) % 2
        rows.append((block * depth + slots[k]).astype(jnp.float32))
    place = jnp.concatenate(
        [picked[0] / total, picked[1] / total] + rows + [jnp.zeros((4, tokens), jnp.float32)],
        axis=0,
    )
    place_ref[...] = place.T
    term = jnp.dot(logit, input_ref[...], preferred_element_type=jnp.float32)
    term_ref[...] = term[:, None, :]


def combine_kernel(cap, place_ref, logit_ref, weight_ref, *refs):
    out_ref = refs[-1]
    depth, part = refs[0].shape[1:]
    tokens = place_ref.shape[0]
    copies = jnp.concatenate([ref[...].reshape(2 * depth, part) for ref in refs[:-1]], axis=0)
    column = lax.broadcasted_iota(jnp.int32, (tokens, copies.shape[0]), 1)
    gates = [place_ref[:, k : k + 1] for k in range(2)]
    base = [place_ref[:, 2 + k : 3 + k].astype(jnp.int32) for k in range(2)]
    for q in range(QUARTERS):
        spread = jnp.where(column == base[0] + q * cap, gates[0], 0.0)
        spread = jnp.where(column == base[1] + q * cap, gates[1], spread)
        high = spread.astype(jnp.bfloat16)
        low = (spread - high.astype(jnp.float32)).astype(jnp.bfloat16)
        both = jnp.dot(
            jnp.concatenate([high, low], axis=0), copies, preferred_element_type=jnp.float32
        )
        columns = slice(q * part, (q + 1) * part)
        total = both[:tokens] + both[tokens:]
        total = total + dot_rows(logit_ref[...], weight_ref[:, columns])
        out_ref[:, columns] = total.astype(jnp.bfloat16)


def shards(side, layer_input, expert_ids, router_probs, router_weight, expert_grads, gate_dots):
    slots, width = expert_grads.shape[2:]
    tokens, experts = router_probs.shape[1:]
    windows = lax.axis_size("exp")
    chips = windows // 2
    cap = slots // windows
    part = width // QUARTERS
    depth = cap * QUARTERS
    params = pltpu.CompilerParams(vmem_limit_bytes=VMEM)

    half = jax.ShapeDtypeStruct((chips, depth, part), jnp.bfloat16)
    kept, given = pl.pallas_call(
        lambda *refs: pack_kernel(cap, *refs),
        out_shape=(half, half),
        grid=(windows // 4,),
        in_specs=[pl.BlockSpec((4 * cap, width), lambda g: (g, 0))],
        out_specs=(pl.BlockSpec((2, depth, part), lambda g: (g, 0, 0)),) * 2,
        compiler_params=params,
    )(expert_grads[0, 0])
    got = lax.ppermute(given, "exp", [(i, i ^ 1) for i in range(windows)])

    laid = pl.pallas_call(
        lambda *refs: gate_pack_kernel(cap, *refs),
        out_shape=jax.ShapeDtypeStruct((windows, 1, LANES), jnp.float32),
        compiler_params=params,
    )(gate_dots[0])
    dots = lax.all_to_all(laid, "exp", 0, 0, tiled=True)

    dealt = pl.pallas_call(
        deal_kernel,
        out_shape=(jax.ShapeDtypeStruct((2, depth, part), jnp.bfloat16),) * chips,
        compiler_params=params,
    )(kept, got)
    copies = [dealt[0]]
    for step, block in zip(STEPS[1:], dealt[1:]):
        moves = [(i, (i + 2 * step) % windows) for i in range(windows)]
        copies.append(lax.ppermute(block, "exp", moves))
    dots, _ = lax.optimization_barrier((dots, dealt))

    ids = jnp.swapaxes(expert_ids, 1, 2)[0]
    probs = jnp.swapaxes(router_probs, 1, 2)[0]
    logit, place, term = pl.pallas_call(
        lambda *refs: router_kernel(depth, *refs),
        out_shape=(
            jax.ShapeDtypeStruct((experts, tokens), jnp.bfloat16),
            jax.ShapeDtypeStruct((tokens, 8), jnp.float32),
            jax.ShapeDtypeStruct((experts, 1, width), jnp.float32),
        ),
        compiler_params=params,
    )(ids, probs, dots, layer_input[0])

    own = jnp.sum(lax.all_to_all(term, "exp", 0, 0, tiled=True), axis=0)
    across = [[x * side + z for x in range(side)] for z in range(side)]
    along = [[x * side + z for z in range(side)] for x in range(side)]
    for groups in (across, along):
        copied = jnp.broadcast_to(own[None], (side,) + own.shape)
        own = jnp.sum(
            lax.all_to_all(copied, "ctx", 0, 0, axis_index_groups=groups, tiled=True), axis=0
        )

    combined = pl.pallas_call(
        lambda *refs: combine_kernel(cap, *refs),
        out_shape=jax.ShapeDtypeStruct((tokens, width), jnp.bfloat16),
        compiler_params=params,
    )(place, logit, router_weight, *copies)
    return combined[None], own


def solution(mesh):
    in_specs = (
        P("exp", "ctx", None),
        P("exp", "ctx", None),
        P("exp", "ctx", None),
        P(),
        P("ctx", "exp", None, None),
        P("ctx", "exp", None),
    )
    out_specs = (P("exp", "ctx", None), P("exp", None))
    side = round(mesh.shape["ctx"] ** 0.5)

    def step(*arrays):
        return shards(side, *arrays)

    return jax.shard_map(step, mesh=mesh, in_specs=in_specs, out_specs=out_specs, check_vma=False)
```

```python
import jax
import jax.numpy as jnp
from jax import lax
from jax.experimental import pallas as pl
from jax.experimental.pallas import tpu as pltpu
from jax.sharding import PartitionSpec as P

QUARTERS = 4
LANES = 128
WHOLE = (0, 3, 5, 4)
SPLIT = (1, 2)
VMEM = 24 * 1024 * 1024


def dot_rows(left, right):
    return lax.dot_general(
        left, right, (((0,), (0,)), ((), ())), preferred_element_type=jnp.float32
    )


def gate_pack_kernel(cap, dots_ref, out_ref):
    windows, lanes = out_ref.shape[0], out_ref.shape[2]
    count = dots_ref.shape[1]
    column = lax.broadcasted_iota(jnp.int32, (windows, count), 1)
    first = lax.broadcasted_iota(jnp.int32, (windows, count), 0) * cap
    dots = jnp.broadcast_to(dots_ref[...].astype(jnp.float32), (windows, count))
    own = jnp.where((column >= first) & (column < first + cap), dots, 0.0)
    slot = lax.broadcasted_iota(jnp.int32, (count, lanes), 0) % cap
    lane = lax.broadcasted_iota(jnp.int32, (count, lanes), 1)
    place = jnp.where(slot == lane, 1.0, 0.0)
    laid = jnp.dot(
        own.astype(jnp.bfloat16), place.astype(jnp.bfloat16), preferred_element_type=jnp.float32
    )
    out_ref[...] = laid[:, None, :]


def split_target(chips, far):
    chip, core = lax.axis_index("exp") // 2, lax.axis_index("exp") % 2
    return (chip + jnp.where(core == 0, far, chips - far)) % chips


def pack_kernel(cap, rows_ref, packed_ref, given_ref):
    part = packed_ref.shape[2]
    chips = packed_ref.shape[0] // 2
    rows = rows_ref[...].astype(jnp.float32)
    for w in range(packed_ref.shape[0]):
        window = rows[w * cap : (w + 1) * cap]
        stacked = jnp.concatenate(
            [window[:, q * part : (q + 1) * part] for q in range(QUARTERS)], axis=0
        )
        packed_ref[w] = stacked.astype(jnp.bfloat16)
    chip, other = lax.axis_index("exp") // 2, 1 - lax.axis_index("exp") % 2
    for n, far in enumerate(WHOLE):
        given_ref[n] = packed_ref[(chip + far) % chips * 2 + other]
    for n, far in enumerate(SPLIT):
        target = (chip + jnp.where(other == 0, far, chips - far)) % chips
        given_ref[len(WHOLE) + 2 * n] = packed_ref[target * 2 + other]
        given_ref[len(WHOLE) + 2 * n + 1] = packed_ref[target * 2 + 1 - other]


def deal_kernel(packed_ref, got_ref, *out_refs):
    chips = packed_ref.shape[0] // 2
    chip, core = lax.axis_index("exp") // 2, lax.axis_index("exp") % 2
    for n, far in enumerate(WHOLE):
        out_refs[n][0] = packed_ref[(chip + far) % chips * 2 + core]
        out_refs[n][1] = got_ref[n]
    for n, far in enumerate(SPLIT):
        out_ref, target = out_refs[len(WHOLE) + n], split_target(chips, far)
        out_ref[0] = packed_ref[target * 2 + core]
        out_ref[1] = got_ref[len(WHOLE) + 2 * n]
        out_ref[2] = packed_ref[target * 2 + 1 - core]
        out_ref[3] = got_ref[len(WHOLE) + 2 * n + 1]


def sum_kernel(parts_ref, out_ref):
    total = parts_ref[0]
    for n in range(1, parts_ref.shape[0]):
        total = total + parts_ref[n]
    for n in range(out_ref.shape[0]):
        out_ref[n] = total


def router_kernel(depth, ids_ref, probs_ref, dots_ref, input_ref, logit_ref, place_ref, term_ref):
    experts, tokens = probs_ref.shape
    probs = probs_ref[...]
    expert = lax.broadcasted_iota(jnp.int32, (experts, tokens), 0)
    chosen = [expert == ids_ref[k : k + 1, :] for k in range(2)]
    mask = jnp.where(chosen[0] | chosen[1], 1.0, 0.0)
    earlier = lax.broadcasted_iota(jnp.int32, (tokens, tokens), 0) < lax.broadcasted_iota(
        jnp.int32, (tokens, tokens), 1
    )
    prior = jnp.dot(
        mask.astype(jnp.bfloat16),
        jnp.where(earlier, 1.0, 0.0).astype(jnp.bfloat16),
        preferred_element_type=jnp.float32,
    )
    dots = dots_ref[...][:, 0, :].astype(jnp.bfloat16)
    lane_count = dots.shape[1]
    slot_row = lax.broadcasted_iota(jnp.int32, (lane_count, tokens), 0)
    picked, gate_grad, slots = [], [], []
    for k in range(2):
        onehot = jnp.where(chosen[k], 1.0, 0.0)
        picked.append(jnp.sum(jnp.where(chosen[k], probs, 0.0), axis=0, keepdims=True))
        slot = jnp.sum(onehot * prior, axis=0, keepdims=True).astype(jnp.int32)
        slots.append(slot)
        values = dot_rows(dots, onehot.astype(jnp.bfloat16))
        gate_grad.append(jnp.sum(jnp.where(slot_row == slot, values, 0.0), axis=0, keepdims=True))
    total = picked[0] + picked[1]
    shared = (gate_grad[0] * picked[0] + gate_grad[1] * picked[1]) / (total * total)
    router_grad = sum(
        jnp.where(chosen[k], gate_grad[k] / total - shared, 0.0) for k in range(2)
    )
    logit = probs * (router_grad - jnp.sum(probs * router_grad, axis=0, keepdims=True))
    logit = logit.astype(jnp.bfloat16)
    logit_ref[...] = logit
    chip, core = lax.axis_index("exp") // 2, lax.axis_index("exp") % 2
    rows = []
    for k in range(2):
        ids = ids_ref[k : k + 1, :]
        step = (chip - ids // 2 + experts // 2) % (experts // 2)
        turned = jnp.where(core == 0, step, (experts // 2 - step) % (experts // 2))
        place = jnp.zeros_like(step)
        for n, far in enumerate(WHOLE):
            place = jnp.where(step == far, n, place)
        for n, far in enumerate(SPLIT):
            place = jnp.where(turned == far, len(WHOLE) + n, place)
            place = jnp.where(
                turned == experts // 2 - far, len(WHOLE) + len(SPLIT) + n, place
            )
        swapped = jnp.where(place >= len(WHOLE) + len(SPLIT), 1, 0)
        block = place * 2 + (ids % 2 + core + swapped) % 2
        rows.append((block * depth + slots[k]).astype(jnp.float32))
    place = jnp.concatenate(
        [picked[0] / total, picked[1] / total] + rows + [jnp.zeros((4, tokens), jnp.float32)],
        axis=0,
    )
    place_ref[...] = place.T
    term = jnp.dot(logit, input_ref[...], preferred_element_type=jnp.float32)
    term_ref[...] = term[:, None, :]


def weighted(cap, place_ref, blocks, first):
    tokens = place_ref.shape[0]
    depth, part = blocks[0].shape[1:]
    copies = jnp.concatenate([block.reshape(2 * depth, part) for block in blocks], axis=0)
    column = lax.broadcasted_iota(jnp.int32, (tokens, copies.shape[0]), 1) + first * depth
    gates = [place_ref[:, k : k + 1] for k in range(2)]
    base = [place_ref[:, 2 + k : 3 + k].astype(jnp.int32) for k in range(2)]
    quarters = []
    for q in range(QUARTERS):
        spread = jnp.where(column == base[0] + q * cap, gates[0], 0.0)
        spread = jnp.where(column == base[1] + q * cap, gates[1], spread)
        high = spread.astype(jnp.bfloat16)
        low = (spread - high.astype(jnp.float32)).astype(jnp.bfloat16)
        both = jnp.dot(
            jnp.concatenate([high, low], axis=0), copies, preferred_element_type=jnp.float32
        )
        quarters.append(both[:tokens] + both[tokens:])
    return quarters


def near_kernel(cap, place_ref, logit_ref, weight_ref, *refs):
    out_ref, near = refs[-1], refs[:-1]
    split = len(SPLIT)
    blocks = [ref[0:2] for ref in near[:split]] + [ref[2:4] for ref in near[split:]]
    part = out_ref.shape[1] // QUARTERS
    for q, total in enumerate(weighted(cap, place_ref, blocks, 2 * len(WHOLE))):
        columns = slice(q * part, (q + 1) * part)
        out_ref[:, columns] = total + dot_rows(logit_ref[...], weight_ref[:, columns])


def far_kernel(cap, place_ref, near_ref, *refs):
    out_ref = refs[-1]
    part = out_ref.shape[1] // QUARTERS
    for q, total in enumerate(weighted(cap, place_ref, [ref[...] for ref in refs[:-1]], 0)):
        columns = slice(q * part, (q + 1) * part)
        out_ref[:, columns] = (total + near_ref[:, columns]).astype(jnp.bfloat16)


def shards(side, layer_input, expert_ids, router_probs, router_weight, expert_grads, gate_dots):
    slots, width = expert_grads.shape[2:]
    tokens, experts = router_probs.shape[1:]
    windows = lax.axis_size("exp")
    chips = windows // 2
    cap = slots // windows
    part = width // QUARTERS
    depth = cap * QUARTERS
    params = pltpu.CompilerParams(vmem_limit_bytes=VMEM)

    def blocks_of(count):
        return jax.ShapeDtypeStruct((count, depth, part), jnp.bfloat16)

    def swap(block):
        return lax.ppermute(block, "exp", [(i, i ^ 1) for i in range(windows)])

    packed, given = pl.pallas_call(
        lambda *refs: pack_kernel(cap, *refs),
        out_shape=(blocks_of(windows), blocks_of(chips)),
        compiler_params=params,
    )(expert_grads[0, 0])
    got = swap(given)

    dealt = pl.pallas_call(
        deal_kernel,
        out_shape=(blocks_of(2),) * len(WHOLE) + (blocks_of(4),) * len(SPLIT),
        compiler_params=params,
    )(packed, got)
    far = [dealt[0]]
    for step, block in zip(WHOLE[1:], dealt[1:]):
        moves = [(i, (i + 2 * step) % windows) for i in range(windows)]
        far.append(lax.ppermute(block, "exp", moves))
    near = []
    for step, block in zip(SPLIT, dealt[len(WHOLE) :]):
        moves = [(i, (i + 2 * (step if i % 2 == 0 else -step)) % windows) for i in range(windows)]
        near.append(lax.ppermute(block, "exp", moves))

    laid = pl.pallas_call(
        lambda *refs: gate_pack_kernel(cap, *refs),
        out_shape=jax.ShapeDtypeStruct((windows, 1, LANES), jnp.float32),
        compiler_params=params,
    )(gate_dots[0])
    ids = jnp.swapaxes(expert_ids, 1, 2)[0]
    probs = jnp.swapaxes(router_probs, 1, 2)[0]

    def add(parts, count):
        return pl.pallas_call(
            sum_kernel,
            out_shape=jax.ShapeDtypeStruct((count, 1, width), jnp.float32),
            compiler_params=params,
        )(parts)

    router_out = (
        jax.ShapeDtypeStruct((experts, tokens), jnp.bfloat16),
        jax.ShapeDtypeStruct((tokens, 8), jnp.float32),
        jax.ShapeDtypeStruct((experts, 1, width), jnp.float32),
    )

    def over_exp(laid):
        dots = lax.all_to_all(laid, "exp", 0, 0, tiled=True)
        logit, place, term = pl.pallas_call(
            lambda *refs: router_kernel(depth, *refs),
            out_shape=router_out,
            compiler_params=params,
        )(ids, probs, dots, layer_input[0])
        return logit, place, add(lax.all_to_all(term, "exp", 0, 0, tiled=True), side)

    def over_ctx(operand):
        own, near = operand
        swapped = [swap(block) for block in near]
        across = [[x * side + z for x in range(side)] for z in range(side)]
        along = [[x * side + z for z in range(side)] for x in range(side)]
        for groups, count in ((across, side), (along, 1)):
            got = lax.all_to_all(own, "ctx", 0, 0, axis_index_groups=groups, tiled=True)
            own = add(got, count)
        return own, swapped

    runs = expert_ids[0, 0, 0] >= 0

    def unit(step, operand):
        out = jax.eval_shape(step, operand)
        empty = lambda _: jax.tree.map(lambda leaf: jnp.zeros(leaf.shape, leaf.dtype), out)
        return lax.cond(runs, step, empty, operand)

    laid, _ = lax.optimization_barrier((laid, dealt))
    logit, place, own = unit(over_exp, laid)
    own, swapped = unit(over_ctx, (own, near))
    near = near + swapped
    place, _ = lax.optimization_barrier((place, own))

    partial = pl.pallas_call(
        lambda *refs: near_kernel(cap, *refs),
        out_shape=jax.ShapeDtypeStruct((tokens, width), jnp.float32),
        compiler_params=params,
    )(place, logit, router_weight, *near)
    combined = pl.pallas_call(
        lambda *refs: far_kernel(cap, *refs),
        out_shape=jax.ShapeDtypeStruct((tokens, width), jnp.bfloat16),
        compiler_params=params,
    )(place, partial, *far)
    return combined[None], own[0]


def solution(mesh):
    in_specs = (
        P("exp", "ctx", None),
        P("exp", "ctx", None),
        P("exp", "ctx", None),
        P(),
        P("ctx", "exp", None, None),
        P("ctx", "exp", None),
    )
    out_specs = (P("exp", "ctx", None), P("exp", None))
    side = round(mesh.shape["ctx"] ** 0.5)

    def step(*arrays):
        return shards(side, *arrays)

    return jax.shard_map(step, mesh=mesh, in_specs=in_specs, out_specs=out_specs, check_vma=False)
```

```python
import jax
import jax.numpy as jnp
from jax import lax
from jax.experimental import pallas as pl
from jax.experimental.pallas import tpu as pltpu
from jax.sharding import PartitionSpec as P

QUARTERS = 4
LANES = 128
WHOLE = (3, 5, 4, 0)
SPLIT = (1, 2)
VMEM = 24 * 1024 * 1024


def dot_rows(left, right):
    return lax.dot_general(
        left, right, (((0,), (0,)), ((), ())), preferred_element_type=jnp.float32
    )


def gate_pack_kernel(cap, dots_ref, out_ref):
    windows, lanes = out_ref.shape[0], out_ref.shape[2]
    count = dots_ref.shape[1]
    column = lax.broadcasted_iota(jnp.int32, (windows, count), 1)
    first = lax.broadcasted_iota(jnp.int32, (windows, count), 0) * cap
    dots = jnp.broadcast_to(dots_ref[...].astype(jnp.float32), (windows, count))
    own = jnp.where((column >= first) & (column < first + cap), dots, 0.0)
    slot = lax.broadcasted_iota(jnp.int32, (count, lanes), 0) % cap
    lane = lax.broadcasted_iota(jnp.int32, (count, lanes), 1)
    place = jnp.where(slot == lane, 1.0, 0.0)
    laid = jnp.dot(
        own.astype(jnp.bfloat16), place.astype(jnp.bfloat16), preferred_element_type=jnp.float32
    )
    out_ref[...] = laid[:, None, :]


def split_target(chips, far):
    chip, core = lax.axis_index("exp") // 2, lax.axis_index("exp") % 2
    return (chip + jnp.where(core == 0, far, chips - far)) % chips


def pack_kernel(cap, rows_ref, packed_ref, given_ref):
    part = packed_ref.shape[2]
    chips = packed_ref.shape[0] // 2
    rows = rows_ref[...].astype(jnp.float32)
    for w in range(packed_ref.shape[0]):
        window = rows[w * cap : (w + 1) * cap]
        stacked = jnp.concatenate(
            [window[:, q * part : (q + 1) * part] for q in range(QUARTERS)], axis=0
        )
        packed_ref[w] = stacked.astype(jnp.bfloat16)
    chip, other = lax.axis_index("exp") // 2, 1 - lax.axis_index("exp") % 2
    for n, far in enumerate(WHOLE):
        given_ref[n] = packed_ref[(chip + far) % chips * 2 + other]
    for n, far in enumerate(SPLIT):
        target = (chip + jnp.where(other == 0, far, chips - far)) % chips
        given_ref[len(WHOLE) + 2 * n] = packed_ref[target * 2 + other]
        given_ref[len(WHOLE) + 2 * n + 1] = packed_ref[target * 2 + 1 - other]


def deal_kernel(packed_ref, got_ref, *out_refs):
    chips = packed_ref.shape[0] // 2
    chip, core = lax.axis_index("exp") // 2, lax.axis_index("exp") % 2
    for n, far in enumerate(WHOLE):
        out_refs[n][0] = packed_ref[(chip + far) % chips * 2 + core]
        out_refs[n][1] = got_ref[n]
    for n, far in enumerate(SPLIT):
        out_ref, target = out_refs[len(WHOLE) + n], split_target(chips, far)
        out_ref[0] = packed_ref[target * 2 + core]
        out_ref[1] = got_ref[len(WHOLE) + 2 * n]
        out_ref[2] = packed_ref[target * 2 + 1 - core]
        out_ref[3] = got_ref[len(WHOLE) + 2 * n + 1]


def sum_kernel(parts_ref, out_ref):
    total = parts_ref[0]
    for n in range(1, parts_ref.shape[0]):
        total = total + parts_ref[n]
    for n in range(out_ref.shape[0]):
        out_ref[n] = total


def router_kernel(depth, ids_ref, probs_ref, dots_ref, input_ref, logit_ref, place_ref, term_ref):
    experts, tokens = probs_ref.shape
    probs = probs_ref[...]
    expert = lax.broadcasted_iota(jnp.int32, (experts, tokens), 0)
    chosen = [expert == ids_ref[k : k + 1, :] for k in range(2)]
    mask = jnp.where(chosen[0] | chosen[1], 1.0, 0.0)
    earlier = lax.broadcasted_iota(jnp.int32, (tokens, tokens), 0) < lax.broadcasted_iota(
        jnp.int32, (tokens, tokens), 1
    )
    prior = jnp.dot(
        mask.astype(jnp.bfloat16),
        jnp.where(earlier, 1.0, 0.0).astype(jnp.bfloat16),
        preferred_element_type=jnp.float32,
    )
    dots = dots_ref[...][:, 0, :].astype(jnp.bfloat16)
    lane_count = dots.shape[1]
    slot_row = lax.broadcasted_iota(jnp.int32, (lane_count, tokens), 0)
    picked, gate_grad, slots = [], [], []
    for k in range(2):
        onehot = jnp.where(chosen[k], 1.0, 0.0)
        picked.append(jnp.sum(jnp.where(chosen[k], probs, 0.0), axis=0, keepdims=True))
        slot = jnp.sum(onehot * prior, axis=0, keepdims=True).astype(jnp.int32)
        slots.append(slot)
        values = dot_rows(dots, onehot.astype(jnp.bfloat16))
        gate_grad.append(jnp.sum(jnp.where(slot_row == slot, values, 0.0), axis=0, keepdims=True))
    total = picked[0] + picked[1]
    shared = (gate_grad[0] * picked[0] + gate_grad[1] * picked[1]) / (total * total)
    router_grad = sum(
        jnp.where(chosen[k], gate_grad[k] / total - shared, 0.0) for k in range(2)
    )
    logit = probs * (router_grad - jnp.sum(probs * router_grad, axis=0, keepdims=True))
    logit = logit.astype(jnp.bfloat16)
    logit_ref[...] = logit
    chip, core = lax.axis_index("exp") // 2, lax.axis_index("exp") % 2
    rows = []
    for k in range(2):
        ids = ids_ref[k : k + 1, :]
        step = (chip - ids // 2 + experts // 2) % (experts // 2)
        turned = jnp.where(core == 0, step, (experts // 2 - step) % (experts // 2))
        place = jnp.zeros_like(step)
        for n, far in enumerate(WHOLE):
            place = jnp.where(step == far, n, place)
        for n, far in enumerate(SPLIT):
            place = jnp.where(turned == far, len(WHOLE) + n, place)
            place = jnp.where(
                turned == experts // 2 - far, len(WHOLE) + len(SPLIT) + n, place
            )
        swapped = jnp.where(place >= len(WHOLE) + len(SPLIT), 1, 0)
        block = place * 2 + (ids % 2 + core + swapped) % 2
        rows.append((block * depth + slots[k]).astype(jnp.float32))
    place = jnp.concatenate(
        [picked[0] / total, picked[1] / total] + rows + [jnp.zeros((4, tokens), jnp.float32)],
        axis=0,
    )
    place_ref[...] = place.T
    term = jnp.dot(logit, input_ref[...], preferred_element_type=jnp.float32)
    term_ref[...] = term[:, None, :]


def weighted(cap, place_ref, blocks, first):
    tokens = place_ref.shape[0]
    depth, part = blocks[0].shape[1:]
    copies = jnp.concatenate([block.reshape(2 * depth, part) for block in blocks], axis=0)
    column = lax.broadcasted_iota(jnp.int32, (tokens, copies.shape[0]), 1) + first * depth
    gates = [place_ref[:, k : k + 1] for k in range(2)]
    base = [place_ref[:, 2 + k : 3 + k].astype(jnp.int32) for k in range(2)]
    quarters = []
    for q in range(QUARTERS):
        spread = jnp.where(column == base[0] + q * cap, gates[0], 0.0)
        spread = jnp.where(column == base[1] + q * cap, gates[1], spread)
        high = spread.astype(jnp.bfloat16)
        low = (spread - high.astype(jnp.float32)).astype(jnp.bfloat16)
        both = jnp.dot(
            jnp.concatenate([high, low], axis=0), copies, preferred_element_type=jnp.float32
        )
        quarters.append(both[:tokens] + both[tokens:])
    return quarters


def near_kernel(cap, place_ref, logit_ref, weight_ref, *refs):
    out_ref, local_ref, near = refs[-1], refs[0], refs[1:-1]
    split = len(SPLIT)
    blocks = [local_ref[...]]
    blocks += [ref[0:2] for ref in near[:split]] + [ref[2:4] for ref in near[split:]]
    part = out_ref.shape[1] // QUARTERS
    for q, total in enumerate(weighted(cap, place_ref, blocks, 2 * len(WHOLE) - 2)):
        columns = slice(q * part, (q + 1) * part)
        out_ref[:, columns] = total + dot_rows(logit_ref[...], weight_ref[:, columns])


def far_kernel(cap, place_ref, near_ref, *refs):
    out_ref = refs[-1]
    part = out_ref.shape[1] // QUARTERS
    for q, total in enumerate(weighted(cap, place_ref, [ref[...] for ref in refs[:-1]], 0)):
        columns = slice(q * part, (q + 1) * part)
        out_ref[:, columns] = (total + near_ref[:, columns]).astype(jnp.bfloat16)


def shards(side, layer_input, expert_ids, router_probs, router_weight, expert_grads, gate_dots):
    slots, width = expert_grads.shape[2:]
    tokens, experts = router_probs.shape[1:]
    windows = lax.axis_size("exp")
    chips = windows // 2
    cap = slots // windows
    part = width // QUARTERS
    depth = cap * QUARTERS
    params = pltpu.CompilerParams(vmem_limit_bytes=VMEM)

    def blocks_of(count):
        return jax.ShapeDtypeStruct((count, depth, part), jnp.bfloat16)

    def swap(block):
        return lax.ppermute(block, "exp", [(i, i ^ 1) for i in range(windows)])

    laid = pl.pallas_call(
        lambda *refs: gate_pack_kernel(cap, *refs),
        out_shape=jax.ShapeDtypeStruct((windows, 1, LANES), jnp.float32),
        compiler_params=params,
    )(gate_dots[0])
    dots = lax.all_to_all(laid, "exp", 0, 0, tiled=True)

    packed, given = pl.pallas_call(
        lambda *refs: pack_kernel(cap, *refs),
        out_shape=(blocks_of(windows), blocks_of(chips)),
        compiler_params=params,
    )(expert_grads[0, 0])
    got, dots = lax.optimization_barrier((swap(given), dots))

    dealt = pl.pallas_call(
        deal_kernel,
        out_shape=(blocks_of(2),) * len(WHOLE) + (blocks_of(4),) * len(SPLIT),
        compiler_params=params,
    )(packed, got)
    far = []
    for step, block in zip(WHOLE[:-1], dealt):
        moves = [(i, (i + 2 * step) % windows) for i in range(windows)]
        far.append(lax.ppermute(block, "exp", moves))
    near = []
    for step, block in zip(SPLIT, dealt[len(WHOLE) :]):
        moves = [(i, (i + 2 * (step if i % 2 == 0 else -step)) % windows) for i in range(windows)]
        near.append(lax.ppermute(block, "exp", moves))

    ids = jnp.swapaxes(expert_ids, 1, 2)[0]
    probs = jnp.swapaxes(router_probs, 1, 2)[0]

    def add(parts, count):
        return pl.pallas_call(
            sum_kernel,
            out_shape=jax.ShapeDtypeStruct((count, 1, width), jnp.float32),
            compiler_params=params,
        )(parts)

    router_out = (
        jax.ShapeDtypeStruct((experts, tokens), jnp.bfloat16),
        jax.ShapeDtypeStruct((tokens, 8), jnp.float32),
        jax.ShapeDtypeStruct((experts, 1, width), jnp.float32),
    )

    def over_exp(dots):
        logit, place, term = pl.pallas_call(
            lambda *refs: router_kernel(depth, *refs),
            out_shape=router_out,
            compiler_params=params,
        )(ids, probs, dots, layer_input[0])
        return logit, place, add(lax.all_to_all(term, "exp", 0, 0, tiled=True), side)

    def over_ctx(operand):
        own, near, *routed = operand
        swapped = [swap(block) for block in near]
        partial = pl.pallas_call(
            lambda *refs: near_kernel(cap, *refs),
            out_shape=jax.ShapeDtypeStruct((tokens, width), jnp.float32),
            compiler_params=params,
        )(*routed, router_weight, dealt[len(WHOLE) - 1], *near, *swapped)
        across = [[x * side + z for x in range(side)] for z in range(side)]
        along = [[x * side + z for z in range(side)] for x in range(side)]
        for groups, count in ((across, side), (along, 1)):
            got = lax.all_to_all(own, "ctx", 0, 0, axis_index_groups=groups, tiled=True)
            own = add(got, count)
        return own, partial

    runs = expert_ids[0, 0, 0] >= 0

    def unit(step, operand):
        out = jax.eval_shape(step, operand)
        empty = lambda _: jax.tree.map(lambda leaf: jnp.zeros(leaf.shape, leaf.dtype), out)
        return lax.cond(runs, step, empty, operand)

    logit, place, own = over_exp(dots)
    own, partial = unit(over_ctx, (own, near, place, logit))
    combined = pl.pallas_call(
        lambda *refs: far_kernel(cap, *refs),
        out_shape=jax.ShapeDtypeStruct((tokens, width), jnp.bfloat16),
        compiler_params=params,
    )(place, partial, *far)
    return combined[None], own[0]


def solution(mesh):
    in_specs = (
        P("exp", "ctx", None),
        P("exp", "ctx", None),
        P("exp", "ctx", None),
        P(),
        P("ctx", "exp", None, None),
        P("ctx", "exp", None),
    )
    out_specs = (P("exp", "ctx", None), P("exp", None))
    side = round(mesh.shape["ctx"] ** 0.5)

    def step(*arrays):
        return shards(side, *arrays)

    return jax.shard_map(step, mesh=mesh, in_specs=in_specs, out_specs=out_specs, check_vma=False)
```

```python
import jax
import jax.numpy as jnp
from jax import lax
from jax.experimental import pallas as pl
from jax.experimental.pallas import tpu as pltpu
from jax.sharding import PartitionSpec as P

QUARTERS = 4
STEPS = (0, 1, 7, 3, 5, 4, 2, 6)
LANES = 128
SUBLANES = 8
VMEM = 24 * 1024 * 1024


def dot_rows(left, right):
    return lax.dot_general(
        left, right, (((0,), (0,)), ((), ())), preferred_element_type=jnp.float32
    )


def gate_pack_kernel(cap, dots_ref, out_ref):
    windows, lanes = out_ref.shape[0], out_ref.shape[2]
    count = dots_ref.shape[1]
    column = lax.broadcasted_iota(jnp.int32, (windows, count), 1)
    first = lax.broadcasted_iota(jnp.int32, (windows, count), 0) * cap
    dots = jnp.broadcast_to(dots_ref[...].astype(jnp.float32), (windows, count))
    own = jnp.where((column >= first) & (column < first + cap), dots, 0.0)
    slot = lax.broadcasted_iota(jnp.int32, (count, lanes), 0) % cap
    lane = lax.broadcasted_iota(jnp.int32, (count, lanes), 1)
    place = jnp.where(slot == lane, 1.0, 0.0)
    laid = jnp.dot(
        own.astype(jnp.bfloat16), place.astype(jnp.bfloat16), preferred_element_type=jnp.float32
    )
    out_ref[...] = laid[:, None, :]


def pack_kernel(cap, rows_ref, kept_ref, given_ref):
    part = kept_ref.shape[2]
    core = lax.axis_index("exp") % 2
    rows = rows_ref[...].astype(jnp.float32)
    for pair in range(kept_ref.shape[0]):
        stacks = []
        for w in (2 * pair, 2 * pair + 1):
            window = rows[w * cap : (w + 1) * cap]
            stacked = jnp.concatenate(
                [window[:, q * part : (q + 1) * part] for q in range(QUARTERS)], axis=0
            )
            stacks.append(stacked)
        kept_ref[pair] = jnp.where(core == 0, stacks[0], stacks[1]).astype(jnp.bfloat16)
        given_ref[pair] = jnp.where(core == 0, stacks[1], stacks[0]).astype(jnp.bfloat16)


def deal_kernel(kept_ref, got_ref, *out_refs):
    chips = kept_ref.shape[0]
    chip = lax.axis_index("exp") // 2
    for step, out_ref in zip(STEPS, out_refs):
        target = (chip + step) % chips
        out_ref[0] = kept_ref[target]
        out_ref[1] = got_ref[target]


def sum_kernel(parts_ref, out_ref):
    total = parts_ref[0]
    for n in range(1, parts_ref.shape[0]):
        total = total + parts_ref[n]
    for n in range(out_ref.shape[0]):
        out_ref[n] = total


def router_kernel(depth, ids_ref, probs_ref, dots_ref, input_ref, logit_ref, place_ref, term_ref):
    experts, tokens = probs_ref.shape
    probs = probs_ref[...]
    expert = lax.broadcasted_iota(jnp.int32, (experts, tokens), 0)
    chosen = [expert == ids_ref[k : k + 1, :] for k in range(2)]
    mask = jnp.where(chosen[0] | chosen[1], 1.0, 0.0)
    earlier = lax.broadcasted_iota(jnp.int32, (tokens, tokens), 0) < lax.broadcasted_iota(
        jnp.int32, (tokens, tokens), 1
    )
    prior = jnp.dot(
        mask.astype(jnp.bfloat16),
        jnp.where(earlier, 1.0, 0.0).astype(jnp.bfloat16),
        preferred_element_type=jnp.float32,
    )
    dots = dots_ref[...][:, 0, :].astype(jnp.bfloat16)
    lane_count = dots.shape[1]
    slot_row = lax.broadcasted_iota(jnp.int32, (lane_count, tokens), 0)
    picked, gate_grad, slots = [], [], []
    for k in range(2):
        onehot = jnp.where(chosen[k], 1.0, 0.0)
        picked.append(jnp.sum(jnp.where(chosen[k], probs, 0.0), axis=0, keepdims=True))
        slot = jnp.sum(onehot * prior, axis=0, keepdims=True).astype(jnp.int32)
        slots.append(slot)
        values = dot_rows(dots, onehot.astype(jnp.bfloat16))
        gate_grad.append(jnp.sum(jnp.where(slot_row == slot, values, 0.0), axis=0, keepdims=True))
    total = picked[0] + picked[1]
    shared = (gate_grad[0] * picked[0] + gate_grad[1] * picked[1]) / (total * total)
    router_grad = sum(
        jnp.where(chosen[k], gate_grad[k] / total - shared, 0.0) for k in range(2)
    )
    logit = probs * (router_grad - jnp.sum(probs * router_grad, axis=0, keepdims=True))
    logit = logit.astype(jnp.bfloat16)
    logit_ref[...] = logit
    chip, core = lax.axis_index("exp") // 2, lax.axis_index("exp") % 2
    rows = []
    for k in range(2):
        ids = ids_ref[k : k + 1, :]
        step = (chip - ids // 2 + experts // 2) % (experts // 2)
        place = sum(jnp.where(step == STEPS[n], n, 0) for n in range(len(STEPS)))
        block = place * 2 + (ids % 2 + core) % 2
        rows.append((block * depth + slots[k]).astype(jnp.float32))
    place = jnp.concatenate(
        [picked[0] / total, picked[1] / total] + rows + [jnp.zeros((4, tokens), jnp.float32)],
        axis=0,
    )
    place_ref[...] = place.T
    term = jnp.dot(logit, input_ref[...], preferred_element_type=jnp.float32)
    term_ref[...] = term[:, None, :]


def combine_kernel(cap, depth, place_ref, logit_ref, weight_ref, *refs):
    out_ref = refs[-1]
    tokens, width = out_ref.shape
    filler = jnp.zeros((depth - cap, width), jnp.float32)
    table = []
    for ref in refs[:-1]:
        for core in range(2):
            stacked = ref[core].astype(jnp.float32)
            rows = [stacked[q * cap : (q + 1) * cap] for q in range(QUARTERS)]
            table += [jnp.concatenate(rows, axis=1), filler]
    copies = jnp.concatenate(table, axis=0).astype(jnp.bfloat16)
    column = lax.broadcasted_iota(jnp.int32, (tokens, copies.shape[0]), 1)
    spread = jnp.zeros(column.shape, jnp.float32)
    for k in range(2):
        base = place_ref[:, 2 + k : 3 + k].astype(jnp.int32)
        spread = jnp.where(column == base, place_ref[:, k : k + 1], spread)
    high = spread.astype(jnp.bfloat16)
    low = (spread - high.astype(jnp.float32)).astype(jnp.bfloat16)
    both = jnp.dot(
        jnp.concatenate([high, low], axis=0), copies, preferred_element_type=jnp.float32
    )
    total = both[:tokens] + both[tokens:] + dot_rows(logit_ref[...], weight_ref[...])
    out_ref[...] = total.astype(jnp.bfloat16)


def shards(side, layer_input, expert_ids, router_probs, router_weight, expert_grads, gate_dots):
    slots, width = expert_grads.shape[2:]
    tokens, experts = router_probs.shape[1:]
    windows = lax.axis_size("exp")
    chips = windows // 2
    cap = slots // windows
    part = width // QUARTERS
    stack = cap * QUARTERS
    depth = -(-cap // SUBLANES) * SUBLANES
    params = pltpu.CompilerParams(vmem_limit_bytes=VMEM)

    runs = expert_ids[0, 0, 0] >= 0

    def unit(step, operand):
        out = jax.eval_shape(step, operand)
        empty = lambda _: jax.tree.map(lambda leaf: jnp.zeros(leaf.shape, leaf.dtype), out)
        return lax.cond(runs, step, empty, operand)

    laid = pl.pallas_call(
        lambda *refs: gate_pack_kernel(cap, *refs),
        out_shape=jax.ShapeDtypeStruct((windows, 1, LANES), jnp.float32),
        compiler_params=params,
    )(gate_dots[0])
    dots = lax.all_to_all(laid, "exp", 0, 0, tiled=True)

    half = jax.ShapeDtypeStruct((chips, stack, part), jnp.bfloat16)

    def share(rows):
        kept, given = pl.pallas_call(
            lambda *refs: pack_kernel(cap, *refs),
            out_shape=(half, half),
            compiler_params=params,
        )(rows)
        return kept, lax.ppermute(given, "exp", [(i, i ^ 1) for i in range(windows)])

    kept, got = unit(share, expert_grads[0, 0])

    ids = jnp.swapaxes(expert_ids, 1, 2)[0]
    probs = jnp.swapaxes(router_probs, 1, 2)[0]
    logit, place, term = pl.pallas_call(
        lambda *refs: router_kernel(depth, *refs),
        out_shape=(
            jax.ShapeDtypeStruct((experts, tokens), jnp.bfloat16),
            jax.ShapeDtypeStruct((tokens, 8), jnp.float32),
            jax.ShapeDtypeStruct((experts, 1, width), jnp.float32),
        ),
        compiler_params=params,
    )(ids, probs, dots, layer_input[0])
    got, term = lax.optimization_barrier((got, term))

    def add(parts, count):
        return pl.pallas_call(
            sum_kernel,
            out_shape=jax.ShapeDtypeStruct((count, 1, width), jnp.float32),
            compiler_params=params,
        )(parts)

    own = add(lax.all_to_all(term, "exp", 0, 0, tiled=True), side)

    dealt = pl.pallas_call(
        deal_kernel,
        out_shape=(jax.ShapeDtypeStruct((2, stack, part), jnp.bfloat16),) * chips,
        compiler_params=params,
    )(kept, got)
    copies = [dealt[0]]
    for step, block in zip(STEPS[1:], dealt[1:]):
        moves = [(i, (i + 2 * step) % windows) for i in range(windows)]
        copies.append(lax.ppermute(block, "exp", moves))

    def over_ctx(own):
        across = [[x * side + z for x in range(side)] for z in range(side)]
        along = [[x * side + z for z in range(side)] for x in range(side)]
        for groups, count in ((across, side), (along, 1)):
            parts = lax.all_to_all(own, "ctx", 0, 0, axis_index_groups=groups, tiled=True)
            own = add(parts, count)
        return own

    own = unit(over_ctx, own)
    place, own = lax.optimization_barrier((place, own))
    combined = pl.pallas_call(
        lambda *refs: combine_kernel(cap, depth, *refs),
        out_shape=jax.ShapeDtypeStruct((tokens, width), jnp.bfloat16),
        compiler_params=params,
    )(place, logit, router_weight, *copies)
    return combined[None], own[0]


def solution(mesh):
    in_specs = (
        P("exp", "ctx", None),
        P("exp", "ctx", None),
        P("exp", "ctx", None),
        P(),
        P("ctx", "exp", None, None),
        P("ctx", "exp", None),
    )
    out_specs = (P("exp", "ctx", None), P("exp", None))
    side = round(mesh.shape["ctx"] ** 0.5)

    def step(*arrays):
        return shards(side, *arrays)

    return jax.shard_map(step, mesh=mesh, in_specs=in_specs, out_specs=out_specs, check_vma=False)
```

```python
import jax
import jax.numpy as jnp
from jax import lax
from jax.experimental import pallas as pl
from jax.experimental.pallas import tpu as pltpu
from jax.sharding import PartitionSpec as P

QUARTERS = 4
STEPS = (3, 5, 1, 7)
LANES = 128
SUBLANES = 8
VMEM = 24 * 1024 * 1024


def dot_rows(left, right):
    return lax.dot_general(
        left, right, (((0,), (0,)), ((), ())), preferred_element_type=jnp.float32
    )


def gate_pack_kernel(cap, dots_ref, out_ref):
    windows, lanes = out_ref.shape[0], out_ref.shape[2]
    count = dots_ref.shape[1]
    column = lax.broadcasted_iota(jnp.int32, (windows, count), 1)
    first = lax.broadcasted_iota(jnp.int32, (windows, count), 0) * cap
    dots = jnp.broadcast_to(dots_ref[...].astype(jnp.float32), (windows, count))
    own = jnp.where((column >= first) & (column < first + cap), dots, 0.0)
    slot = lax.broadcasted_iota(jnp.int32, (count, lanes), 0) % cap
    lane = lax.broadcasted_iota(jnp.int32, (count, lanes), 1)
    place = jnp.where(slot == lane, 1.0, 0.0)
    laid = jnp.dot(
        own.astype(jnp.bfloat16), place.astype(jnp.bfloat16), preferred_element_type=jnp.float32
    )
    out_ref[...] = laid[:, None, :]


def pack_kernel(cap, rows_ref, even_ref, kept_ref, given_ref):
    part = even_ref.shape[2]
    chip, core = lax.axis_index("exp") // 2, lax.axis_index("exp") % 2
    rows = rows_ref[...].astype(jnp.float32)
    for group in range(kept_ref.shape[0]):
        stacks = []
        for w in range(4 * group, 4 * group + 4):
            window = rows[w * cap : (w + 1) * cap]
            stacked = jnp.concatenate(
                [window[:, q * part : (q + 1) * part] for q in range(QUARTERS)], axis=0
            )
            stacks.append(stacked)
        same = chip % 2 == 0
        for n in range(2):
            even = jnp.where(same, stacks[n], stacks[2 + n])
            even_ref[2 * group + n] = even.astype(jnp.bfloat16)
        odd = [jnp.where(same, stacks[2 + n], stacks[n]) for n in range(2)]
        kept_ref[group] = jnp.where(core == 0, odd[0], odd[1]).astype(jnp.bfloat16)
        given_ref[group] = jnp.where(core == 0, odd[1], odd[0]).astype(jnp.bfloat16)


def deal_kernel(kept_ref, got_ref, *out_refs):
    chips = 2 * kept_ref.shape[0]
    chip = lax.axis_index("exp") // 2
    for step, out_ref in zip(STEPS, out_refs):
        target = (chip + step) % chips // 2
        out_ref[0] = kept_ref[target]
        out_ref[1] = got_ref[target]


def sum_kernel(parts_ref, out_ref):
    total = parts_ref[0]
    for n in range(1, parts_ref.shape[0]):
        total = total + parts_ref[n]
    for n in range(out_ref.shape[0]):
        out_ref[n] = total


def router_kernel(depth, ids_ref, probs_ref, dots_ref, input_ref, logit_ref, place_ref, term_ref):
    experts, tokens = probs_ref.shape
    probs = probs_ref[...]
    expert = lax.broadcasted_iota(jnp.int32, (experts, tokens), 0)
    chosen = [expert == ids_ref[k : k + 1, :] for k in range(2)]
    mask = jnp.where(chosen[0] | chosen[1], 1.0, 0.0)
    earlier = lax.broadcasted_iota(jnp.int32, (tokens, tokens), 0) < lax.broadcasted_iota(
        jnp.int32, (tokens, tokens), 1
    )
    prior = jnp.dot(
        mask.astype(jnp.bfloat16),
        jnp.where(earlier, 1.0, 0.0).astype(jnp.bfloat16),
        preferred_element_type=jnp.float32,
    )
    dots = dots_ref[...][:, 0, :].astype(jnp.bfloat16)
    lane_count = dots.shape[1]
    slot_row = lax.broadcasted_iota(jnp.int32, (lane_count, tokens), 0)
    picked, gate_grad, slots = [], [], []
    for k in range(2):
        onehot = jnp.where(chosen[k], 1.0, 0.0)
        picked.append(jnp.sum(jnp.where(chosen[k], probs, 0.0), axis=0, keepdims=True))
        slot = jnp.sum(onehot * prior, axis=0, keepdims=True).astype(jnp.int32)
        slots.append(slot)
        values = dot_rows(dots, onehot.astype(jnp.bfloat16))
        gate_grad.append(jnp.sum(jnp.where(slot_row == slot, values, 0.0), axis=0, keepdims=True))
    total = picked[0] + picked[1]
    shared = (gate_grad[0] * picked[0] + gate_grad[1] * picked[1]) / (total * total)
    router_grad = sum(
        jnp.where(chosen[k], gate_grad[k] / total - shared, 0.0) for k in range(2)
    )
    logit = probs * (router_grad - jnp.sum(probs * router_grad, axis=0, keepdims=True))
    logit = logit.astype(jnp.bfloat16)
    logit_ref[...] = logit
    chip, core = lax.axis_index("exp") // 2, lax.axis_index("exp") % 2
    rows = []
    for k in range(2):
        ids = ids_ref[k : k + 1, :]
        step = (chip - ids // 2 + experts // 2) % (experts // 2)
        place = sum(jnp.where(step == STEPS[n], n, 0) for n in range(len(STEPS)))
        odd = place * 2 + (ids % 2 + core) % 2
        block = jnp.where(step % 2 == 1, odd, experts // 2 + ids // 4 * 2 + ids % 2)
        rows.append((block * depth + slots[k]).astype(jnp.float32))
    place = jnp.concatenate(
        [picked[0] / total, picked[1] / total] + rows + [jnp.zeros((4, tokens), jnp.float32)],
        axis=0,
    )
    place_ref[...] = place.T
    term = jnp.dot(logit, input_ref[...], preferred_element_type=jnp.float32)
    term_ref[...] = term[:, None, :]


def combine_kernel(cap, depth, place_ref, logit_ref, weight_ref, *refs):
    out_ref = refs[-1]
    tokens, width = out_ref.shape
    filler = jnp.zeros((depth - cap, width), jnp.float32)
    table = []
    for ref in refs[:-1]:
        for n in range(ref.shape[0]):
            stacked = ref[n].astype(jnp.float32)
            rows = [stacked[q * cap : (q + 1) * cap] for q in range(QUARTERS)]
            table += [jnp.concatenate(rows, axis=1), filler]
    copies = jnp.concatenate(table, axis=0).astype(jnp.bfloat16)
    column = lax.broadcasted_iota(jnp.int32, (tokens, copies.shape[0]), 1)
    spread = jnp.zeros(column.shape, jnp.float32)
    for k in range(2):
        base = place_ref[:, 2 + k : 3 + k].astype(jnp.int32)
        spread = jnp.where(column == base, place_ref[:, k : k + 1], spread)
    high = spread.astype(jnp.bfloat16)
    low = (spread - high.astype(jnp.float32)).astype(jnp.bfloat16)
    both = jnp.dot(
        jnp.concatenate([high, low], axis=0), copies, preferred_element_type=jnp.float32
    )
    total = both[:tokens] + both[tokens:] + dot_rows(logit_ref[...], weight_ref[...])
    out_ref[...] = total.astype(jnp.bfloat16)


def shards(side, layer_input, expert_ids, router_probs, router_weight, expert_grads, gate_dots):
    slots, width = expert_grads.shape[2:]
    tokens, experts = router_probs.shape[1:]
    windows = lax.axis_size("exp")
    chips = windows // 2
    cap = slots // windows
    part = width // QUARTERS
    stack = cap * QUARTERS
    depth = -(-cap // SUBLANES) * SUBLANES
    params = pltpu.CompilerParams(vmem_limit_bytes=VMEM)

    runs = expert_ids[0, 0, 0] >= 0

    def unit(step, operand):
        out = jax.eval_shape(step, operand)
        empty = lambda _: jax.tree.map(lambda leaf: jnp.zeros(leaf.shape, leaf.dtype), out)
        return lax.cond(runs, step, empty, operand)

    laid = pl.pallas_call(
        lambda *refs: gate_pack_kernel(cap, *refs),
        out_shape=jax.ShapeDtypeStruct((windows, 1, LANES), jnp.float32),
        compiler_params=params,
    )(gate_dots[0])
    dots = lax.all_to_all(laid, "exp", 0, 0, tiled=True)

    def blocks_of(count):
        return jax.ShapeDtypeStruct((count, stack, part), jnp.bfloat16)

    def share(rows):
        even, kept, given = pl.pallas_call(
            lambda *refs: pack_kernel(cap, *refs),
            out_shape=(blocks_of(chips), blocks_of(chips // 2), blocks_of(chips // 2)),
            compiler_params=params,
        )(rows)
        return even, kept, lax.ppermute(given, "exp", [(i, i ^ 1) for i in range(windows)])

    even, kept, got = unit(share, expert_grads[0, 0])

    ids = jnp.swapaxes(expert_ids, 1, 2)[0]
    probs = jnp.swapaxes(router_probs, 1, 2)[0]
    logit, place, term = pl.pallas_call(
        lambda *refs: router_kernel(depth, *refs),
        out_shape=(
            jax.ShapeDtypeStruct((experts, tokens), jnp.bfloat16),
            jax.ShapeDtypeStruct((tokens, 8), jnp.float32),
            jax.ShapeDtypeStruct((experts, 1, width), jnp.float32),
        ),
        compiler_params=params,
    )(ids, probs, dots, layer_input[0])
    got, term = lax.optimization_barrier((got, term))

    def add(parts, count):
        return pl.pallas_call(
            sum_kernel,
            out_shape=jax.ShapeDtypeStruct((count, 1, width), jnp.float32),
            compiler_params=params,
        )(parts)

    own = add(lax.all_to_all(term, "exp", 0, 0, tiled=True), 1)

    dealt = pl.pallas_call(
        deal_kernel,
        out_shape=(blocks_of(2),) * len(STEPS),
        compiler_params=params,
    )(kept, got)
    copies = []
    for step, block in zip(STEPS, dealt):
        moves = [(i, (i + 2 * step) % windows) for i in range(windows)]
        copies.append(lax.ppermute(block, "exp", moves))
    alike = [[i for i in range(windows) if i // 2 % 2 == parity] for parity in range(2)]
    even, own, *copies[:2] = lax.optimization_barrier((even, own, *copies[:2]))
    copies.append(lax.all_to_all(even, "exp", 0, 0, axis_index_groups=alike, tiled=True))

    def over_ctx(own):
        bit = 1
        while bit < side * side:
            moves = [(i, i ^ bit) for i in range(side * side)]
            own = own + lax.ppermute(own, "ctx", moves)
            bit *= 2
        return own

    own = unit(over_ctx, own)
    place, own = lax.optimization_barrier((place, own))
    combined = pl.pallas_call(
        lambda *refs: combine_kernel(cap, depth, *refs),
        out_shape=jax.ShapeDtypeStruct((tokens, width), jnp.bfloat16),
        compiler_params=params,
    )(place, logit, router_weight, *copies)
    return combined[None], own[0]


def solution(mesh):
    in_specs = (
        P("exp", "ctx", None),
        P("exp", "ctx", None),
        P("exp", "ctx", None),
        P(),
        P("ctx", "exp", None, None),
        P("ctx", "exp", None),
    )
    out_specs = (P("exp", "ctx", None), P("exp", None))
    side = round(mesh.shape["ctx"] ** 0.5)

    def step(*arrays):
        return shards(side, *arrays)

    return jax.shard_map(step, mesh=mesh, in_specs=in_specs, out_specs=out_specs, check_vma=False)
```

```python
import jax
import jax.numpy as jnp
from jax import lax
from jax.experimental import pallas as pl
from jax.experimental.pallas import tpu as pltpu
from jax.sharding import PartitionSpec as P

QUARTERS = 4
STEPS = (0, 3, 5, 2, 6, 4, 1, 7)
LANES = 128
SUBLANES = 8
VMEM = 24 * 1024 * 1024


def dot_rows(left, right):
    return lax.dot_general(
        left, right, (((0,), (0,)), ((), ())), preferred_element_type=jnp.float32
    )


def gate_pack_kernel(cap, dots_ref, out_ref):
    windows, lanes = out_ref.shape[0], out_ref.shape[2]
    count = dots_ref.shape[1]
    column = lax.broadcasted_iota(jnp.int32, (windows, count), 1)
    first = lax.broadcasted_iota(jnp.int32, (windows, count), 0) * cap
    dots = jnp.broadcast_to(dots_ref[...].astype(jnp.float32), (windows, count))
    own = jnp.where((column >= first) & (column < first + cap), dots, 0.0)
    slot = lax.broadcasted_iota(jnp.int32, (count, lanes), 0) % cap
    lane = lax.broadcasted_iota(jnp.int32, (count, lanes), 1)
    place = jnp.where(slot == lane, 1.0, 0.0)
    laid = jnp.dot(
        own.astype(jnp.bfloat16), place.astype(jnp.bfloat16), preferred_element_type=jnp.float32
    )
    out_ref[...] = laid[:, None, :]


def pack_kernel(cap, rows_ref, kept_ref, given_ref):
    part = kept_ref.shape[2]
    core = lax.axis_index("exp") % 2
    rows = rows_ref[...].astype(jnp.float32)
    for pair in range(kept_ref.shape[0]):
        stacks = []
        for w in (2 * pair, 2 * pair + 1):
            window = rows[w * cap : (w + 1) * cap]
            stacked = jnp.concatenate(
                [window[:, q * part : (q + 1) * part] for q in range(QUARTERS)], axis=0
            )
            stacks.append(stacked)
        kept_ref[pair] = jnp.where(core == 0, stacks[0], stacks[1]).astype(jnp.bfloat16)
        given_ref[pair] = jnp.where(core == 0, stacks[1], stacks[0]).astype(jnp.bfloat16)


def deal_kernel(kept_ref, got_ref, *out_refs):
    chips = kept_ref.shape[0]
    chip = lax.axis_index("exp") // 2
    for step, out_ref in zip(STEPS, out_refs):
        target = (chip + step) % chips
        out_ref[0] = kept_ref[target]
        out_ref[1] = got_ref[target]


def sum_kernel(parts_ref, out_ref):
    total = parts_ref[0]
    for n in range(1, parts_ref.shape[0]):
        total = total + parts_ref[n]
    for n in range(out_ref.shape[0]):
        out_ref[n] = total


def router_kernel(depth, ids_ref, probs_ref, dots_ref, input_ref, logit_ref, place_ref, term_ref):
    experts, tokens = probs_ref.shape
    probs = probs_ref[...]
    expert = lax.broadcasted_iota(jnp.int32, (experts, tokens), 0)
    chosen = [expert == ids_ref[k : k + 1, :] for k in range(2)]
    mask = jnp.where(chosen[0] | chosen[1], 1.0, 0.0)
    earlier = lax.broadcasted_iota(jnp.int32, (tokens, tokens), 0) < lax.broadcasted_iota(
        jnp.int32, (tokens, tokens), 1
    )
    prior = jnp.dot(
        mask.astype(jnp.bfloat16),
        jnp.where(earlier, 1.0, 0.0).astype(jnp.bfloat16),
        preferred_element_type=jnp.float32,
    )
    dots = dots_ref[...][:, 0, :].astype(jnp.bfloat16)
    lane_count = dots.shape[1]
    slot_row = lax.broadcasted_iota(jnp.int32, (lane_count, tokens), 0)
    picked, gate_grad, slots = [], [], []
    for k in range(2):
        onehot = jnp.where(chosen[k], 1.0, 0.0)
        picked.append(jnp.sum(jnp.where(chosen[k], probs, 0.0), axis=0, keepdims=True))
        slot = jnp.sum(onehot * prior, axis=0, keepdims=True).astype(jnp.int32)
        slots.append(slot)
        values = dot_rows(dots, onehot.astype(jnp.bfloat16))
        gate_grad.append(jnp.sum(jnp.where(slot_row == slot, values, 0.0), axis=0, keepdims=True))
    total = picked[0] + picked[1]
    shared = (gate_grad[0] * picked[0] + gate_grad[1] * picked[1]) / (total * total)
    router_grad = sum(
        jnp.where(chosen[k], gate_grad[k] / total - shared, 0.0) for k in range(2)
    )
    logit = probs * (router_grad - jnp.sum(probs * router_grad, axis=0, keepdims=True))
    logit = logit.astype(jnp.bfloat16)
    logit_ref[...] = logit
    chip, core = lax.axis_index("exp") // 2, lax.axis_index("exp") % 2
    rows = []
    for k in range(2):
        ids = ids_ref[k : k + 1, :]
        step = (chip - ids // 2 + experts // 2) % (experts // 2)
        place = sum(jnp.where(step == STEPS[n], n, 0) for n in range(len(STEPS)))
        block = place * 2 + (ids % 2 + core) % 2
        rows.append((block * depth + slots[k]).astype(jnp.float32))
    place = jnp.concatenate(
        [picked[0] / total, picked[1] / total] + rows + [jnp.zeros((4, tokens), jnp.float32)],
        axis=0,
    )
    place_ref[...] = place.T
    term = jnp.dot(logit, input_ref[...], preferred_element_type=jnp.float32)
    term_ref[...] = term[:, None, :]


def combine_kernel(cap, depth, place_ref, logit_ref, weight_ref, *refs):
    out_ref = refs[-1]
    tokens, width = out_ref.shape
    filler = jnp.zeros((depth - cap, width), jnp.float32)
    table = []
    for ref in refs[:-1]:
        for core in range(2):
            stacked = ref[core].astype(jnp.float32)
            rows = [stacked[q * cap : (q + 1) * cap] for q in range(QUARTERS)]
            table += [jnp.concatenate(rows, axis=1), filler]
    copies = jnp.concatenate(table, axis=0).astype(jnp.bfloat16)
    column = lax.broadcasted_iota(jnp.int32, (tokens, copies.shape[0]), 1)
    spread = jnp.zeros(column.shape, jnp.float32)
    for k in range(2):
        base = place_ref[:, 2 + k : 3 + k].astype(jnp.int32)
        spread = jnp.where(column == base, place_ref[:, k : k + 1], spread)
    high = spread.astype(jnp.bfloat16)
    low = (spread - high.astype(jnp.float32)).astype(jnp.bfloat16)
    both = jnp.dot(
        jnp.concatenate([high, low], axis=0), copies, preferred_element_type=jnp.float32
    )
    total = both[:tokens] + both[tokens:] + dot_rows(logit_ref[...], weight_ref[...])
    out_ref[...] = total.astype(jnp.bfloat16)


def shards(side, layer_input, expert_ids, router_probs, router_weight, expert_grads, gate_dots):
    slots, width = expert_grads.shape[2:]
    tokens, experts = router_probs.shape[1:]
    windows = lax.axis_size("exp")
    chips = windows // 2
    cap = slots // windows
    part = width // QUARTERS
    stack = cap * QUARTERS
    depth = -(-cap // SUBLANES) * SUBLANES
    params = pltpu.CompilerParams(vmem_limit_bytes=VMEM)

    runs = expert_ids[0, 0, 0] >= 0

    def unit(step, operand):
        out = jax.eval_shape(step, operand)
        empty = lambda _: jax.tree.map(lambda leaf: jnp.zeros(leaf.shape, leaf.dtype), out)
        return lax.cond(runs, step, empty, operand)

    laid = pl.pallas_call(
        lambda *refs: gate_pack_kernel(cap, *refs),
        out_shape=jax.ShapeDtypeStruct((windows, 1, LANES), jnp.float32),
        compiler_params=params,
    )(gate_dots[0])
    dots = lax.all_to_all(laid, "exp", 0, 0, tiled=True)

    half = jax.ShapeDtypeStruct((chips, stack, part), jnp.bfloat16)

    def share(rows):
        kept, given = pl.pallas_call(
            lambda *refs: pack_kernel(cap, *refs),
            out_shape=(half, half),
            compiler_params=params,
        )(rows)
        return kept, lax.ppermute(given, "exp", [(i, i ^ 1) for i in range(windows)])

    kept, got = unit(share, expert_grads[0, 0])

    ids = jnp.swapaxes(expert_ids, 1, 2)[0]
    probs = jnp.swapaxes(router_probs, 1, 2)[0]
    logit, place, term = pl.pallas_call(
        lambda *refs: router_kernel(depth, *refs),
        out_shape=(
            jax.ShapeDtypeStruct((experts, tokens), jnp.bfloat16),
            jax.ShapeDtypeStruct((tokens, 8), jnp.float32),
            jax.ShapeDtypeStruct((experts, 1, width), jnp.float32),
        ),
        compiler_params=params,
    )(ids, probs, dots, layer_input[0])
    got, term = lax.optimization_barrier((got, term))

    def add(parts, count):
        return pl.pallas_call(
            sum_kernel,
            out_shape=jax.ShapeDtypeStruct((count, 1, width), jnp.float32),
            compiler_params=params,
        )(parts)

    dealt = pl.pallas_call(
        deal_kernel,
        out_shape=(jax.ShapeDtypeStruct((2, stack, part), jnp.bfloat16),) * chips,
        compiler_params=params,
    )(kept, got)
    across = [[x * side + z for x in range(side)] for z in range(side)]
    along = [[x * side + z for z in range(side)] for x in range(side)]
    copies, first = [dealt[0]], 1
    own = term
    for count, axis, groups, number in (
        (side, "exp", None, 2),
        (side, "ctx", across, 3),
        (1, "ctx", along, 2),
    ):
        *blocks, own = lax.optimization_barrier((*dealt[first : first + number], own))
        parts = lax.all_to_all(own, axis, 0, 0, axis_index_groups=groups, tiled=True)
        for step, block in zip(STEPS[first:], blocks):
            moves = [(i, (i + 2 * step) % windows) for i in range(windows)]
            copies.append(lax.ppermute(block, "exp", moves))
        own = add(parts, count)
        first += number

    combined = pl.pallas_call(
        lambda *refs: combine_kernel(cap, depth, *refs),
        out_shape=jax.ShapeDtypeStruct((tokens, width), jnp.bfloat16),
        compiler_params=params,
    )(place, logit, router_weight, *copies)
    return combined[None], own[0]


def solution(mesh):
    in_specs = (
        P("exp", "ctx", None),
        P("exp", "ctx", None),
        P("exp", "ctx", None),
        P(),
        P("ctx", "exp", None, None),
        P("ctx", "exp", None),
    )
    out_specs = (P("exp", "ctx", None), P("exp", None))
    side = round(mesh.shape["ctx"] ** 0.5)

    def step(*arrays):
        return shards(side, *arrays)

    return jax.shard_map(step, mesh=mesh, in_specs=in_specs, out_specs=out_specs, check_vma=False)
```

```python
import jax
import jax.numpy as jnp
from jax import lax
from jax.experimental import pallas as pl
from jax.experimental.pallas import tpu as pltpu
from jax.sharding import PartitionSpec as P

QUARTERS = 4
LANES = 128
SUBLANES = 8
VMEM = 24 * 1024 * 1024


def dot_rows(left, right):
    return lax.dot_general(
        left, right, (((0,), (0,)), ((), ())), preferred_element_type=jnp.float32
    )


def gate_pack_kernel(cap, dots_ref, out_ref):
    windows, lanes = out_ref.shape[0], out_ref.shape[2]
    count = dots_ref.shape[1]
    column = lax.broadcasted_iota(jnp.int32, (windows, count), 1)
    first = lax.broadcasted_iota(jnp.int32, (windows, count), 0) * cap
    dots = jnp.broadcast_to(dots_ref[...].astype(jnp.float32), (windows, count))
    own = jnp.where((column >= first) & (column < first + cap), dots, 0.0)
    slot = lax.broadcasted_iota(jnp.int32, (count, lanes), 0) % cap
    lane = lax.broadcasted_iota(jnp.int32, (count, lanes), 1)
    place = jnp.where(slot == lane, 1.0, 0.0)
    laid = jnp.dot(
        own.astype(jnp.bfloat16), place.astype(jnp.bfloat16), preferred_element_type=jnp.float32
    )
    out_ref[...] = laid[:, None, :]


def pack_kernel(cap, rows_ref, out_ref):
    part = out_ref.shape[2]
    rows = rows_ref[...].astype(jnp.float32)
    for w in range(out_ref.shape[0]):
        window = rows[w * cap : (w + 1) * cap]
        stacked = jnp.concatenate(
            [window[:, q * part : (q + 1) * part] for q in range(QUARTERS)], axis=0
        )
        out_ref[w] = stacked.astype(jnp.bfloat16)


def sum_kernel(parts_ref, out_ref):
    total = parts_ref[0]
    for n in range(1, parts_ref.shape[0]):
        total = total + parts_ref[n]
    for n in range(out_ref.shape[0]):
        out_ref[n] = total


def router_kernel(depth, ids_ref, probs_ref, dots_ref, input_ref, logit_ref, place_ref, term_ref):
    experts, tokens = probs_ref.shape
    probs = probs_ref[...]
    expert = lax.broadcasted_iota(jnp.int32, (experts, tokens), 0)
    chosen = [expert == ids_ref[k : k + 1, :] for k in range(2)]
    mask = jnp.where(chosen[0] | chosen[1], 1.0, 0.0)
    earlier = lax.broadcasted_iota(jnp.int32, (tokens, tokens), 0) < lax.broadcasted_iota(
        jnp.int32, (tokens, tokens), 1
    )
    prior = jnp.dot(
        mask.astype(jnp.bfloat16),
        jnp.where(earlier, 1.0, 0.0).astype(jnp.bfloat16),
        preferred_element_type=jnp.float32,
    )
    dots = dots_ref[...][:, 0, :].astype(jnp.bfloat16)
    lane_count = dots.shape[1]
    slot_row = lax.broadcasted_iota(jnp.int32, (lane_count, tokens), 0)
    picked, gate_grad, slots = [], [], []
    for k in range(2):
        onehot = jnp.where(chosen[k], 1.0, 0.0)
        picked.append(jnp.sum(jnp.where(chosen[k], probs, 0.0), axis=0, keepdims=True))
        slot = jnp.sum(onehot * prior, axis=0, keepdims=True).astype(jnp.int32)
        slots.append(slot)
        values = dot_rows(dots, onehot.astype(jnp.bfloat16))
        gate_grad.append(jnp.sum(jnp.where(slot_row == slot, values, 0.0), axis=0, keepdims=True))
    total = picked[0] + picked[1]
    shared = (gate_grad[0] * picked[0] + gate_grad[1] * picked[1]) / (total * total)
    router_grad = sum(
        jnp.where(chosen[k], gate_grad[k] / total - shared, 0.0) for k in range(2)
    )
    logit = probs * (router_grad - jnp.sum(probs * router_grad, axis=0, keepdims=True))
    logit = logit.astype(jnp.bfloat16)
    logit_ref[...] = logit
    rows = []
    for k in range(2):
        block = ids_ref[k : k + 1, :]
        rows.append((block * depth + slots[k]).astype(jnp.float32))
    place = jnp.concatenate(
        [picked[0] / total, picked[1] / total] + rows + [jnp.zeros((4, tokens), jnp.float32)],
        axis=0,
    )
    place_ref[...] = place.T
    term = jnp.dot(logit, input_ref[...], preferred_element_type=jnp.float32)
    term_ref[...] = term[:, None, :]


def combine_kernel(cap, depth, place_ref, logit_ref, weight_ref, copies_ref, out_ref):
    tokens, width = out_ref.shape
    filler = jnp.zeros((depth - cap, width), jnp.float32)
    table = []
    for expert in range(copies_ref.shape[0]):
        stacked = copies_ref[expert].astype(jnp.float32)
        rows = [stacked[q * cap : (q + 1) * cap] for q in range(QUARTERS)]
        table += [jnp.concatenate(rows, axis=1), filler]
    copies = jnp.concatenate(table, axis=0).astype(jnp.bfloat16)
    column = lax.broadcasted_iota(jnp.int32, (tokens, copies.shape[0]), 1)
    spread = jnp.zeros(column.shape, jnp.float32)
    for k in range(2):
        base = place_ref[:, 2 + k : 3 + k].astype(jnp.int32)
        spread = jnp.where(column == base, place_ref[:, k : k + 1], spread)
    high = spread.astype(jnp.bfloat16)
    low = (spread - high.astype(jnp.float32)).astype(jnp.bfloat16)
    both = jnp.dot(
        jnp.concatenate([high, low], axis=0), copies, preferred_element_type=jnp.float32
    )
    total = both[:tokens] + both[tokens:] + dot_rows(logit_ref[...], weight_ref[...])
    out_ref[...] = total.astype(jnp.bfloat16)


def shards(side, layer_input, expert_ids, router_probs, router_weight, expert_grads, gate_dots):
    slots, width = expert_grads.shape[2:]
    tokens, experts = router_probs.shape[1:]
    windows = lax.axis_size("exp")
    cap = slots // windows
    part = width // QUARTERS
    stack = cap * QUARTERS
    depth = -(-cap // SUBLANES) * SUBLANES
    params = pltpu.CompilerParams(vmem_limit_bytes=VMEM)

    runs = expert_ids[0, 0, 0] >= 0

    def unit(step, operand):
        out = jax.eval_shape(step, operand)
        empty = lambda _: jax.tree.map(lambda leaf: jnp.zeros(leaf.shape, leaf.dtype), out)
        return lax.cond(runs, step, empty, operand)

    laid = pl.pallas_call(
        lambda *refs: gate_pack_kernel(cap, *refs),
        out_shape=jax.ShapeDtypeStruct((windows, 1, LANES), jnp.float32),
        compiler_params=params,
    )(gate_dots[0])
    dots = lax.all_to_all(laid, "exp", 0, 0, tiled=True)

    packed = pl.pallas_call(
        lambda *refs: pack_kernel(cap, *refs),
        out_shape=jax.ShapeDtypeStruct((windows, stack, part), jnp.bfloat16),
        compiler_params=params,
    )(expert_grads[0, 0])

    dots, packed = lax.optimization_barrier((dots, packed))
    ids = jnp.swapaxes(expert_ids, 1, 2)[0]
    probs = jnp.swapaxes(router_probs, 1, 2)[0]
    logit, place, term = pl.pallas_call(
        lambda *refs: router_kernel(depth, *refs),
        out_shape=(
            jax.ShapeDtypeStruct((experts, tokens), jnp.bfloat16),
            jax.ShapeDtypeStruct((tokens, 8), jnp.float32),
            jax.ShapeDtypeStruct((experts, 1, width), jnp.float32),
        ),
        compiler_params=params,
    )(ids, probs, dots, layer_input[0])
    def add(parts, count):
        return pl.pallas_call(
            sum_kernel,
            out_shape=jax.ShapeDtypeStruct((count, 1, width), jnp.float32),
            compiler_params=params,
        )(parts)

    own = add(lax.all_to_all(term, "exp", 0, 0, tiled=True), 1)

    packed, own = lax.optimization_barrier((packed, own))
    copies = lax.all_to_all(packed, "exp", 0, 0, tiled=True)

    def over_ctx(own):
        bit = 1
        while bit < side * side:
            moves = [(i, i ^ bit) for i in range(side * side)]
            own = own + lax.ppermute(own, "ctx", moves)
            bit *= 2
        return own

    own = unit(over_ctx, own)
    place, own = lax.optimization_barrier((place, own))
    combined = pl.pallas_call(
        lambda *refs: combine_kernel(cap, depth, *refs),
        out_shape=jax.ShapeDtypeStruct((tokens, width), jnp.bfloat16),
        compiler_params=params,
    )(place, logit, router_weight, copies)
    return combined[None], own[0]


def solution(mesh):
    in_specs = (
        P("exp", "ctx", None),
        P("exp", "ctx", None),
        P("exp", "ctx", None),
        P(),
        P("ctx", "exp", None, None),
        P("ctx", "exp", None),
    )
    out_specs = (P("exp", "ctx", None), P("exp", None))
    side = round(mesh.shape["ctx"] ** 0.5)

    def step(*arrays):
        return shards(side, *arrays)

    return jax.shard_map(step, mesh=mesh, in_specs=in_specs, out_specs=out_specs, check_vma=False)
```

```python
import jax
import jax.numpy as jnp
from jax import lax
from jax.experimental import pallas as pl
from jax.experimental.pallas import tpu as pltpu
from jax.sharding import PartitionSpec as P

QUARTERS = 4
LANES = 128
SUBLANES = 8
TILE = 16
VMEM = 24 * 1024 * 1024


def dot_rows(left, right):
    return lax.dot_general(
        left, right, (((0,), (0,)), ((), ())), preferred_element_type=jnp.float32
    )


def gate_pack_kernel(cap, dots_ref, out_ref):
    windows, lanes = out_ref.shape[0], out_ref.shape[2]
    count = dots_ref.shape[1]
    column = lax.broadcasted_iota(jnp.int32, (windows, count), 1)
    first = lax.broadcasted_iota(jnp.int32, (windows, count), 0) * cap
    dots = jnp.broadcast_to(dots_ref[...].astype(jnp.float32), (windows, count))
    own = jnp.where((column >= first) & (column < first + cap), dots, 0.0)
    slot = lax.broadcasted_iota(jnp.int32, (count, lanes), 0) % cap
    lane = lax.broadcasted_iota(jnp.int32, (count, lanes), 1)
    place = jnp.where(slot == lane, 1.0, 0.0)
    laid = jnp.dot(
        own.astype(jnp.bfloat16), place.astype(jnp.bfloat16), preferred_element_type=jnp.float32
    )
    out_ref[...] = laid[:, None, :]


def pack_kernel(cap, rows_ref, out_ref):
    part = out_ref.shape[2]
    rows = rows_ref[...].astype(jnp.float32)
    for w in range(out_ref.shape[0]):
        window = rows[w * cap : (w + 1) * cap]
        stacked = jnp.concatenate(
            [window[:, q * part : (q + 1) * part] for q in range(QUARTERS)], axis=0
        )
        out_ref[w] = stacked.astype(jnp.bfloat16)


def sum_kernel(parts_ref, out_ref):
    total = parts_ref[0]
    for n in range(1, parts_ref.shape[0]):
        total = total + parts_ref[n]
    for n in range(out_ref.shape[0]):
        out_ref[n] = total


def router_kernel(depth, ids_ref, probs_ref, dots_ref, input_ref, logit_ref, place_ref, term_ref):
    experts, tokens = probs_ref.shape
    probs = probs_ref[...]
    expert = lax.broadcasted_iota(jnp.int32, (experts, tokens), 0)
    chosen = [expert == ids_ref[k : k + 1, :] for k in range(2)]
    mask = jnp.where(chosen[0] | chosen[1], 1.0, 0.0)
    earlier = lax.broadcasted_iota(jnp.int32, (tokens, tokens), 0) < lax.broadcasted_iota(
        jnp.int32, (tokens, tokens), 1
    )
    prior = jnp.dot(
        mask.astype(jnp.bfloat16),
        jnp.where(earlier, 1.0, 0.0).astype(jnp.bfloat16),
        preferred_element_type=jnp.float32,
    )
    dots = dots_ref[...][:, 0, :].astype(jnp.bfloat16)
    lane_count = dots.shape[1]
    slot_row = lax.broadcasted_iota(jnp.int32, (lane_count, tokens), 0)
    picked, gate_grad, slots = [], [], []
    for k in range(2):
        onehot = jnp.where(chosen[k], 1.0, 0.0)
        picked.append(jnp.sum(jnp.where(chosen[k], probs, 0.0), axis=0, keepdims=True))
        slot = jnp.sum(onehot * prior, axis=0, keepdims=True).astype(jnp.int32)
        slots.append(slot)
        values = dot_rows(dots, onehot.astype(jnp.bfloat16))
        gate_grad.append(jnp.sum(jnp.where(slot_row == slot, values, 0.0), axis=0, keepdims=True))
    total = picked[0] + picked[1]
    shared = (gate_grad[0] * picked[0] + gate_grad[1] * picked[1]) / (total * total)
    router_grad = sum(
        jnp.where(chosen[k], gate_grad[k] / total - shared, 0.0) for k in range(2)
    )
    logit = probs * (router_grad - jnp.sum(probs * router_grad, axis=0, keepdims=True))
    logit = logit.astype(jnp.bfloat16)
    logit_ref[...] = logit
    rows = []
    for k in range(2):
        block = ids_ref[k : k + 1, :]
        rows.append((block * depth + slots[k]).astype(jnp.float32))
    place = jnp.concatenate(
        [picked[0] / total, picked[1] / total] + rows + [jnp.zeros((4, tokens), jnp.float32)],
        axis=0,
    )
    place_ref[...] = place.T
    term = jnp.dot(logit, input_ref[...], preferred_element_type=jnp.float32)
    term_ref[...] = term[:, None, :]


def spread_kernel(slots, place_ref, logit_ref, out_ref):
    tokens = place_ref.shape[0]
    column = lax.broadcasted_iota(jnp.int32, (tokens, slots), 1)
    spread = jnp.zeros(column.shape, jnp.float32)
    for k in range(2):
        base = place_ref[:, 2 + k : 3 + k].astype(jnp.int32)
        spread = jnp.where(column == base, place_ref[:, k : k + 1], spread)
    high = spread.astype(jnp.bfloat16)
    low = (spread - high.astype(jnp.float32)).astype(jnp.bfloat16)
    out_ref[:tokens, :slots] = high
    out_ref[tokens:, :slots] = low
    logit = logit_ref[...].astype(jnp.float32).T.astype(jnp.bfloat16)
    out_ref[:tokens, slots:] = logit
    out_ref[tokens:, slots:] = jnp.zeros_like(logit)


def combine_kernel(cap, depth, spread_ref, weight_ref, copies_ref, out_ref, held, sems):
    tokens = out_ref.shape[0]
    part = copies_ref.shape[2]
    filler = jnp.zeros((depth - cap, part), jnp.float32)
    writes = []
    for q in range(QUARTERS):
        table = []
        start = q * cap // TILE * TILE
        stop = -(-(q + 1) * cap // TILE) * TILE
        for expert in range(copies_ref.shape[0]):
            rows = copies_ref[expert, start:stop, :].astype(jnp.float32)
            table += [rows[q * cap - start : (q + 1) * cap - start], filler]
        columns = slice(q * part, (q + 1) * part)
        copies = jnp.concatenate(table, axis=0).astype(jnp.bfloat16)
        right = jnp.concatenate([copies, weight_ref[:, columns]], axis=0)
        both = jnp.dot(spread_ref[...], right, preferred_element_type=jnp.float32)
        held[q] = (both[:tokens] + both[tokens:]).astype(jnp.bfloat16)
        write = pltpu.make_async_copy(held.at[q], out_ref.at[:, columns], sems.at[q])
        write.start()
        writes.append(write)
    for write in writes:
        write.wait()


def shards(side, layer_input, expert_ids, router_probs, router_weight, expert_grads, gate_dots):
    slots, width = expert_grads.shape[2:]
    tokens, experts = router_probs.shape[1:]
    windows = lax.axis_size("exp")
    cap = slots // windows
    part = width // QUARTERS
    stack = cap * QUARTERS
    depth = -(-cap // SUBLANES) * SUBLANES
    params = pltpu.CompilerParams(vmem_limit_bytes=VMEM)

    runs = expert_ids[0, 0, 0] >= 0

    def unit(step, operand):
        out = jax.eval_shape(step, operand)
        empty = lambda _: jax.tree.map(lambda leaf: jnp.zeros(leaf.shape, leaf.dtype), out)
        return lax.cond(runs, step, empty, operand)

    laid = pl.pallas_call(
        lambda *refs: gate_pack_kernel(cap, *refs),
        out_shape=jax.ShapeDtypeStruct((windows, 1, LANES), jnp.float32),
        compiler_params=params,
    )(gate_dots[0])
    dots = lax.all_to_all(laid, "exp", 0, 0, tiled=True)

    packed = pl.pallas_call(
        lambda *refs: pack_kernel(cap, *refs),
        out_shape=jax.ShapeDtypeStruct((windows, stack, part), jnp.bfloat16),
        compiler_params=params,
    )(expert_grads[0, 0])

    dots, packed = lax.optimization_barrier((dots, packed))
    ids = jnp.swapaxes(expert_ids, 1, 2)[0]
    probs = jnp.swapaxes(router_probs, 1, 2)[0]
    logit, place, term = pl.pallas_call(
        lambda *refs: router_kernel(depth, *refs),
        out_shape=(
            jax.ShapeDtypeStruct((experts, tokens), jnp.bfloat16),
            jax.ShapeDtypeStruct((tokens, 8), jnp.float32),
            jax.ShapeDtypeStruct((experts, 1, width), jnp.float32),
        ),
        compiler_params=params,
    )(ids, probs, dots, layer_input[0])
    def add(parts, count):
        return pl.pallas_call(
            sum_kernel,
            out_shape=jax.ShapeDtypeStruct((count, 1, width), jnp.float32),
            compiler_params=params,
        )(parts)

    own = add(lax.all_to_all(term, "exp", 0, 0, tiled=True), 1)

    packed, own = lax.optimization_barrier((packed, own))
    copies = lax.all_to_all(packed, "exp", 0, 0, tiled=True)

    def over_ctx(operand):
        own, place, logit = operand
        spread = pl.pallas_call(
            lambda *refs: spread_kernel(experts * depth, *refs),
            out_shape=jax.ShapeDtypeStruct((2 * tokens, experts * (depth + 1)), jnp.bfloat16),
            compiler_params=params,
        )(place, logit)
        bit = 1
        while bit < side * side:
            moves = [(i, i ^ bit) for i in range(side * side)]
            own = own + lax.ppermute(own, "ctx", moves)
            bit *= 2
        return own, spread

    own, spread = unit(over_ctx, (own, place, logit))
    combined = pl.pallas_call(
        lambda *refs: combine_kernel(cap, depth, *refs),
        out_shape=jax.ShapeDtypeStruct((tokens, width), jnp.bfloat16),
        out_specs=pl.BlockSpec(memory_space=pl.ANY),
        scratch_shapes=[
            pltpu.VMEM((QUARTERS, tokens, part), jnp.bfloat16),
            pltpu.SemaphoreType.DMA((QUARTERS,)),
        ],
        compiler_params=params,
    )(spread, router_weight, copies)
    return combined[None], own[0]


def solution(mesh):
    in_specs = (
        P("exp", "ctx", None),
        P("exp", "ctx", None),
        P("exp", "ctx", None),
        P(),
        P("ctx", "exp", None, None),
        P("ctx", "exp", None),
    )
    out_specs = (P("exp", "ctx", None), P("exp", None))
    side = round(mesh.shape["ctx"] ** 0.5)

    def step(*arrays):
        return shards(side, *arrays)

    return jax.shard_map(step, mesh=mesh, in_specs=in_specs, out_specs=out_specs, check_vma=False)
```

```python
import jax
import jax.numpy as jnp
from jax import lax
from jax.experimental import pallas as pl
from jax.experimental.pallas import tpu as pltpu
from jax.sharding import PartitionSpec as P

QUARTERS = 4
LANES = 128
SUBLANES = 8
TILE = 16
VMEM = 24 * 1024 * 1024


def dot_rows(left, right):
    return lax.dot_general(
        left, right, (((0,), (0,)), ((), ())), preferred_element_type=jnp.float32
    )


def gate_pack_kernel(cap, dots_ref, out_ref):
    windows, lanes = out_ref.shape[0], out_ref.shape[2]
    count = dots_ref.shape[1]
    column = lax.broadcasted_iota(jnp.int32, (windows, count), 1)
    first = lax.broadcasted_iota(jnp.int32, (windows, count), 0) * cap
    dots = jnp.broadcast_to(dots_ref[...].astype(jnp.float32), (windows, count))
    own = jnp.where((column >= first) & (column < first + cap), dots, 0.0)
    slot = lax.broadcasted_iota(jnp.int32, (count, lanes), 0) % cap
    lane = lax.broadcasted_iota(jnp.int32, (count, lanes), 1)
    place = jnp.where(slot == lane, 1.0, 0.0)
    laid = jnp.dot(
        own.astype(jnp.bfloat16), place.astype(jnp.bfloat16), preferred_element_type=jnp.float32
    )
    out_ref[...] = laid[:, None, :]


def pack_kernel(cap, rows_ref, kept_ref, given_ref):
    part = kept_ref.shape[2]
    core = lax.axis_index("exp") % 2
    rows = rows_ref[...].astype(jnp.float32)
    for pair in range(kept_ref.shape[0]):
        stacks = []
        for w in (2 * pair, 2 * pair + 1):
            window = rows[w * cap : (w + 1) * cap]
            stacked = jnp.concatenate(
                [window[:, q * part : (q + 1) * part] for q in range(QUARTERS)], axis=0
            )
            stacks.append(stacked)
        kept_ref[pair] = jnp.where(core == 0, stacks[0], stacks[1]).astype(jnp.bfloat16)
        given_ref[pair] = jnp.where(core == 0, stacks[1], stacks[0]).astype(jnp.bfloat16)


def deal_kernel(kept_ref, got_ref, out_ref):
    for chip in range(kept_ref.shape[0]):
        out_ref[2 * chip] = kept_ref[chip]
        out_ref[2 * chip + 1] = got_ref[chip]


def sum_kernel(parts_ref, out_ref):
    total = parts_ref[0]
    for n in range(1, parts_ref.shape[0]):
        total = total + parts_ref[n]
    for n in range(out_ref.shape[0]):
        out_ref[n] = total


def router_kernel(depth, ids_ref, probs_ref, dots_ref, input_ref, logit_ref, place_ref, term_ref):
    experts, tokens = probs_ref.shape
    probs = probs_ref[...]
    expert = lax.broadcasted_iota(jnp.int32, (experts, tokens), 0)
    chosen = [expert == ids_ref[k : k + 1, :] for k in range(2)]
    mask = jnp.where(chosen[0] | chosen[1], 1.0, 0.0)
    earlier = lax.broadcasted_iota(jnp.int32, (tokens, tokens), 0) < lax.broadcasted_iota(
        jnp.int32, (tokens, tokens), 1
    )
    prior = jnp.dot(
        mask.astype(jnp.bfloat16),
        jnp.where(earlier, 1.0, 0.0).astype(jnp.bfloat16),
        preferred_element_type=jnp.float32,
    )
    dots = dots_ref[...][:, 0, :].astype(jnp.bfloat16)
    lane_count = dots.shape[1]
    slot_row = lax.broadcasted_iota(jnp.int32, (lane_count, tokens), 0)
    picked, gate_grad, slots = [], [], []
    for k in range(2):
        onehot = jnp.where(chosen[k], 1.0, 0.0)
        picked.append(jnp.sum(jnp.where(chosen[k], probs, 0.0), axis=0, keepdims=True))
        slot = jnp.sum(onehot * prior, axis=0, keepdims=True).astype(jnp.int32)
        slots.append(slot)
        values = dot_rows(dots, onehot.astype(jnp.bfloat16))
        gate_grad.append(jnp.sum(jnp.where(slot_row == slot, values, 0.0), axis=0, keepdims=True))
    total = picked[0] + picked[1]
    shared = (gate_grad[0] * picked[0] + gate_grad[1] * picked[1]) / (total * total)
    router_grad = sum(
        jnp.where(chosen[k], gate_grad[k] / total - shared, 0.0) for k in range(2)
    )
    logit = probs * (router_grad - jnp.sum(probs * router_grad, axis=0, keepdims=True))
    logit = logit.astype(jnp.bfloat16)
    logit_ref[...] = logit
    core = lax.axis_index("exp") % 2
    rows = []
    for k in range(2):
        ids = ids_ref[k : k + 1, :]
        block = ids // 2 * 2 + (ids % 2 + core) % 2
        rows.append((block * depth + slots[k]).astype(jnp.float32))
    place = jnp.concatenate(
        [picked[0] / total, picked[1] / total] + rows + [jnp.zeros((4, tokens), jnp.float32)],
        axis=0,
    )
    place_ref[...] = place.T
    term = jnp.dot(logit, input_ref[...], preferred_element_type=jnp.float32)
    term_ref[...] = term[:, None, :]


def spread_kernel(slots, place_ref, logit_ref, out_ref):
    tokens = place_ref.shape[0]
    column = lax.broadcasted_iota(jnp.int32, (tokens, slots), 1)
    spread = jnp.zeros(column.shape, jnp.float32)
    for k in range(2):
        base = place_ref[:, 2 + k : 3 + k].astype(jnp.int32)
        spread = jnp.where(column == base, place_ref[:, k : k + 1], spread)
    high = spread.astype(jnp.bfloat16)
    low = (spread - high.astype(jnp.float32)).astype(jnp.bfloat16)
    out_ref[:tokens, :slots] = high
    out_ref[tokens:, :slots] = low
    logit = logit_ref[...].astype(jnp.float32).T.astype(jnp.bfloat16)
    out_ref[:tokens, slots:] = logit
    out_ref[tokens:, slots:] = jnp.zeros_like(logit)


def combine_kernel(cap, depth, spread_ref, weight_ref, copies_ref, out_ref, held, sems):
    tokens = out_ref.shape[0]
    part = copies_ref.shape[2]
    filler = jnp.zeros((depth - cap, part), jnp.float32)
    writes = []
    for q in range(QUARTERS):
        table = []
        start = q * cap // TILE * TILE
        stop = -(-(q + 1) * cap // TILE) * TILE
        for expert in range(copies_ref.shape[0]):
            rows = copies_ref[expert, start:stop, :].astype(jnp.float32)
            table += [rows[q * cap - start : (q + 1) * cap - start], filler]
        columns = slice(q * part, (q + 1) * part)
        copies = jnp.concatenate(table, axis=0).astype(jnp.bfloat16)
        right = jnp.concatenate([copies, weight_ref[:, columns]], axis=0)
        both = jnp.dot(spread_ref[...], right, preferred_element_type=jnp.float32)
        held[q] = (both[:tokens] + both[tokens:]).astype(jnp.bfloat16)
        write = pltpu.make_async_copy(held.at[q], out_ref.at[:, columns], sems.at[q])
        write.start()
        writes.append(write)
    for write in writes:
        write.wait()


def shards(side, layer_input, expert_ids, router_probs, router_weight, expert_grads, gate_dots):
    slots, width = expert_grads.shape[2:]
    tokens, experts = router_probs.shape[1:]
    windows = lax.axis_size("exp")
    cap = slots // windows
    part = width // QUARTERS
    stack = cap * QUARTERS
    depth = -(-cap // SUBLANES) * SUBLANES
    params = pltpu.CompilerParams(vmem_limit_bytes=VMEM)

    runs = expert_ids[0, 0, 0] >= 0

    def unit(step, operand):
        out = jax.eval_shape(step, operand)
        empty = lambda _: jax.tree.map(lambda leaf: jnp.zeros(leaf.shape, leaf.dtype), out)
        return lax.cond(runs, step, empty, operand)

    laid = pl.pallas_call(
        lambda *refs: gate_pack_kernel(cap, *refs),
        out_shape=jax.ShapeDtypeStruct((windows, 1, LANES), jnp.float32),
        compiler_params=params,
    )(gate_dots[0])
    dots = lax.all_to_all(laid, "exp", 0, 0, tiled=True)

    half = jax.ShapeDtypeStruct((windows // 2, stack, part), jnp.bfloat16)

    def share(rows):
        kept, given = pl.pallas_call(
            lambda *refs: pack_kernel(cap, *refs),
            out_shape=(half, half),
            compiler_params=params,
        )(rows)
        return kept, lax.ppermute(given, "exp", [(i, i ^ 1) for i in range(windows)])

    kept, got = unit(share, expert_grads[0, 0])
    dots, got = lax.optimization_barrier((dots, got))
    ids = jnp.swapaxes(expert_ids, 1, 2)[0]
    probs = jnp.swapaxes(router_probs, 1, 2)[0]
    logit, place, term = pl.pallas_call(
        lambda *refs: router_kernel(depth, *refs),
        out_shape=(
            jax.ShapeDtypeStruct((experts, tokens), jnp.bfloat16),
            jax.ShapeDtypeStruct((tokens, 8), jnp.float32),
            jax.ShapeDtypeStruct((experts, 1, width), jnp.float32),
        ),
        compiler_params=params,
    )(ids, probs, dots, layer_input[0])
    def add(parts, count):
        return pl.pallas_call(
            sum_kernel,
            out_shape=jax.ShapeDtypeStruct((count, 1, width), jnp.float32),
            compiler_params=params,
        )(parts)

    own = add(lax.all_to_all(term, "exp", 0, 0, tiled=True), 1)

    dealt = pl.pallas_call(
        deal_kernel,
        out_shape=jax.ShapeDtypeStruct((windows, stack, part), jnp.bfloat16),
        compiler_params=params,
    )(kept, got)
    dealt, own = lax.optimization_barrier((dealt, own))
    cores = [[i for i in range(windows) if i % 2 == core] for core in range(2)]
    copies = lax.all_to_all(dealt, "exp", 0, 0, axis_index_groups=cores, tiled=True)

    def over_ctx(operand):
        own, place, logit = operand
        spread = pl.pallas_call(
            lambda *refs: spread_kernel(experts * depth, *refs),
            out_shape=jax.ShapeDtypeStruct((2 * tokens, experts * (depth + 1)), jnp.bfloat16),
            compiler_params=params,
        )(place, logit)
        bit = 1
        while bit < side * side:
            moves = [(i, i ^ bit) for i in range(side * side)]
            own = own + lax.ppermute(own, "ctx", moves)
            bit *= 2
        return own, spread

    own, spread = unit(over_ctx, (own, place, logit))
    combined = pl.pallas_call(
        lambda *refs: combine_kernel(cap, depth, *refs),
        out_shape=jax.ShapeDtypeStruct((tokens, width), jnp.bfloat16),
        out_specs=pl.BlockSpec(memory_space=pl.ANY),
        scratch_shapes=[
            pltpu.VMEM((QUARTERS, tokens, part), jnp.bfloat16),
            pltpu.SemaphoreType.DMA((QUARTERS,)),
        ],
        compiler_params=params,
    )(spread, router_weight, copies)
    return combined[None], own[0]


def solution(mesh):
    in_specs = (
        P("exp", "ctx", None),
        P("exp", "ctx", None),
        P("exp", "ctx", None),
        P(),
        P("ctx", "exp", None, None),
        P("ctx", "exp", None),
    )
    out_specs = (P("exp", "ctx", None), P("exp", None))
    side = round(mesh.shape["ctx"] ** 0.5)

    def step(*arrays):
        return shards(side, *arrays)

    return jax.shard_map(step, mesh=mesh, in_specs=in_specs, out_specs=out_specs, check_vma=False)
```

```python
import jax
import jax.numpy as jnp
from jax import lax
from jax.experimental import pallas as pl
from jax.experimental.pallas import tpu as pltpu
from jax.sharding import PartitionSpec as P

QUARTERS = 4
LANES = 128
SUBLANES = 8
TILE = 16
VMEM = 24 * 1024 * 1024


def dot_rows(left, right):
    return lax.dot_general(
        left, right, (((0,), (0,)), ((), ())), preferred_element_type=jnp.float32
    )


def gate_pack_kernel(cap, dots_ref, out_ref):
    windows, lanes = out_ref.shape[0], out_ref.shape[2]
    count = dots_ref.shape[1]
    column = lax.broadcasted_iota(jnp.int32, (windows, count), 1)
    first = lax.broadcasted_iota(jnp.int32, (windows, count), 0) * cap
    dots = jnp.broadcast_to(dots_ref[...].astype(jnp.float32), (windows, count))
    own = jnp.where((column >= first) & (column < first + cap), dots, 0.0)
    slot = lax.broadcasted_iota(jnp.int32, (count, lanes), 0) % cap
    lane = lax.broadcasted_iota(jnp.int32, (count, lanes), 1)
    place = jnp.where(slot == lane, 1.0, 0.0)
    laid = jnp.dot(
        own.astype(jnp.bfloat16), place.astype(jnp.bfloat16), preferred_element_type=jnp.float32
    )
    out_ref[...] = laid[:, None, :]


def pack_kernel(cap, rows_ref, kept_ref, given_ref):
    part = kept_ref.shape[2]
    core = lax.axis_index("exp") % 2
    rows = rows_ref[...].astype(jnp.float32)
    for pair in range(kept_ref.shape[0]):
        stacks = []
        for w in (2 * pair, 2 * pair + 1):
            window = rows[w * cap : (w + 1) * cap]
            stacked = jnp.concatenate(
                [window[:, q * part : (q + 1) * part] for q in range(QUARTERS)], axis=0
            )
            stacks.append(stacked)
        kept_ref[pair] = jnp.where(core == 0, stacks[0], stacks[1]).astype(jnp.bfloat16)
        given_ref[pair] = jnp.where(core == 0, stacks[1], stacks[0]).astype(jnp.bfloat16)


def deal_kernel(kept_ref, got_ref, out_ref):
    stack = kept_ref.shape[1]
    for chip in range(kept_ref.shape[0]):
        out_ref[chip, :stack, :] = kept_ref[chip]
        out_ref[chip, stack:, :] = got_ref[chip]


def sum_kernel(parts_ref, out_ref):
    total = parts_ref[0]
    for n in range(1, parts_ref.shape[0]):
        total = total + parts_ref[n]
    for n in range(out_ref.shape[0]):
        out_ref[n] = total


def router_kernel(depth, ids_ref, probs_ref, dots_ref, input_ref, logit_ref, place_ref, term_ref):
    experts, tokens = probs_ref.shape
    probs = probs_ref[...]
    expert = lax.broadcasted_iota(jnp.int32, (experts, tokens), 0)
    chosen = [expert == ids_ref[k : k + 1, :] for k in range(2)]
    mask = jnp.where(chosen[0] | chosen[1], 1.0, 0.0)
    earlier = lax.broadcasted_iota(jnp.int32, (tokens, tokens), 0) < lax.broadcasted_iota(
        jnp.int32, (tokens, tokens), 1
    )
    prior = jnp.dot(
        mask.astype(jnp.bfloat16),
        jnp.where(earlier, 1.0, 0.0).astype(jnp.bfloat16),
        preferred_element_type=jnp.float32,
    )
    dots = dots_ref[...][:, 0, :].astype(jnp.bfloat16)
    lane_count = dots.shape[1]
    slot_row = lax.broadcasted_iota(jnp.int32, (lane_count, tokens), 0)
    picked, gate_grad, slots = [], [], []
    for k in range(2):
        onehot = jnp.where(chosen[k], 1.0, 0.0)
        picked.append(jnp.sum(jnp.where(chosen[k], probs, 0.0), axis=0, keepdims=True))
        slot = jnp.sum(onehot * prior, axis=0, keepdims=True).astype(jnp.int32)
        slots.append(slot)
        values = dot_rows(dots, onehot.astype(jnp.bfloat16))
        gate_grad.append(jnp.sum(jnp.where(slot_row == slot, values, 0.0), axis=0, keepdims=True))
    total = picked[0] + picked[1]
    shared = (gate_grad[0] * picked[0] + gate_grad[1] * picked[1]) / (total * total)
    router_grad = sum(
        jnp.where(chosen[k], gate_grad[k] / total - shared, 0.0) for k in range(2)
    )
    logit = probs * (router_grad - jnp.sum(probs * router_grad, axis=0, keepdims=True))
    logit = logit.astype(jnp.bfloat16)
    logit_ref[...] = logit
    core = lax.axis_index("exp") % 2
    rows = []
    for k in range(2):
        ids = ids_ref[k : k + 1, :]
        block = ids // 2 * 2 + (ids % 2 + core) % 2
        rows.append((block * depth + slots[k]).astype(jnp.float32))
    place = jnp.concatenate(
        [picked[0] / total, picked[1] / total] + rows + [jnp.zeros((4, tokens), jnp.float32)],
        axis=0,
    )
    place_ref[...] = place.T
    term = jnp.dot(logit, input_ref[...], preferred_element_type=jnp.float32)
    term_ref[...] = term[:, None, :]


def spread_kernel(slots, place_ref, logit_ref, out_ref):
    tokens = place_ref.shape[0]
    column = lax.broadcasted_iota(jnp.int32, (tokens, slots), 1)
    spread = jnp.zeros(column.shape, jnp.float32)
    for k in range(2):
        base = place_ref[:, 2 + k : 3 + k].astype(jnp.int32)
        spread = jnp.where(column == base, place_ref[:, k : k + 1], spread)
    high = spread.astype(jnp.bfloat16)
    low = (spread - high.astype(jnp.float32)).astype(jnp.bfloat16)
    out_ref[:tokens, :slots] = high
    out_ref[tokens:, :slots] = low
    logit = logit_ref[...].astype(jnp.float32).T.astype(jnp.bfloat16)
    out_ref[:tokens, slots:] = logit
    out_ref[tokens:, slots:] = jnp.zeros_like(logit)


def combine_kernel(cap, depth, spread_ref, weight_ref, copies_ref, out_ref, held, sems):
    tokens = out_ref.shape[0]
    part = copies_ref.shape[2]
    filler = jnp.zeros((depth - cap, part), jnp.float32)
    writes = []
    for q in range(QUARTERS):
        table = []
        start = q * cap // TILE * TILE
        stop = -(-(q + 1) * cap // TILE) * TILE
        for expert in range(copies_ref.shape[0]):
            rows = copies_ref[expert, start:stop, :].astype(jnp.float32)
            table += [rows[q * cap - start : (q + 1) * cap - start], filler]
        columns = slice(q * part, (q + 1) * part)
        copies = jnp.concatenate(table, axis=0).astype(jnp.bfloat16)
        right = jnp.concatenate([copies, weight_ref[:, columns]], axis=0)
        both = jnp.dot(spread_ref[...], right, preferred_element_type=jnp.float32)
        held[q] = (both[:tokens] + both[tokens:]).astype(jnp.bfloat16)
        write = pltpu.make_async_copy(held.at[q], out_ref.at[:, columns], sems.at[q])
        write.start()
        writes.append(write)
    for write in writes:
        write.wait()


def shards(side, layer_input, expert_ids, router_probs, router_weight, expert_grads, gate_dots):
    slots, width = expert_grads.shape[2:]
    tokens, experts = router_probs.shape[1:]
    windows = lax.axis_size("exp")
    cap = slots // windows
    part = width // QUARTERS
    stack = cap * QUARTERS
    depth = -(-cap // SUBLANES) * SUBLANES
    params = pltpu.CompilerParams(vmem_limit_bytes=VMEM)

    runs = expert_ids[0, 0, 0] >= 0

    def unit(step, operand):
        out = jax.eval_shape(step, operand)
        empty = lambda _: jax.tree.map(lambda leaf: jnp.zeros(leaf.shape, leaf.dtype), out)
        return lax.cond(runs, step, empty, operand)

    laid = pl.pallas_call(
        lambda *refs: gate_pack_kernel(cap, *refs),
        out_shape=jax.ShapeDtypeStruct((windows, 1, LANES), jnp.float32),
        compiler_params=params,
    )(gate_dots[0])
    dots = lax.all_to_all(laid, "exp", 0, 0, tiled=True)

    half = jax.ShapeDtypeStruct((windows // 2, stack, part), jnp.bfloat16)

    def share(rows):
        kept, given = pl.pallas_call(
            lambda *refs: pack_kernel(cap, *refs),
            out_shape=(half, half),
            compiler_params=params,
        )(rows)
        return kept, lax.ppermute(given, "exp", [(i, i ^ 1) for i in range(windows)])

    kept, got = unit(share, expert_grads[0, 0])
    dots, got = lax.optimization_barrier((dots, got))
    ids = jnp.swapaxes(expert_ids, 1, 2)[0]
    probs = jnp.swapaxes(router_probs, 1, 2)[0]
    logit, place, term = pl.pallas_call(
        lambda *refs: router_kernel(depth, *refs),
        out_shape=(
            jax.ShapeDtypeStruct((experts, tokens), jnp.bfloat16),
            jax.ShapeDtypeStruct((tokens, 8), jnp.float32),
            jax.ShapeDtypeStruct((experts, 1, width), jnp.float32),
        ),
        compiler_params=params,
    )(ids, probs, dots, layer_input[0])
    dealt = pl.pallas_call(
        deal_kernel,
        out_shape=jax.ShapeDtypeStruct((windows // 2, 2 * stack, part), jnp.bfloat16),
        compiler_params=params,
    )(kept, got)
    term, dealt = lax.optimization_barrier((term, dealt))

    def add(parts, count):
        return pl.pallas_call(
            sum_kernel,
            out_shape=jax.ShapeDtypeStruct((count, 1, width), jnp.float32),
            compiler_params=params,
        )(parts)

    own = add(lax.all_to_all(term, "exp", 0, 0, tiled=True), 1)

    dealt, own = lax.optimization_barrier((dealt, own))
    cores = [[i for i in range(windows) if i % 2 == core] for core in range(2)]
    copies = lax.all_to_all(dealt, "exp", 0, 0, axis_index_groups=cores, tiled=True)
    copies = copies.reshape(windows, stack, part)

    def over_ctx(operand):
        own, place, logit = operand
        spread = pl.pallas_call(
            lambda *refs: spread_kernel(experts * depth, *refs),
            out_shape=jax.ShapeDtypeStruct((2 * tokens, experts * (depth + 1)), jnp.bfloat16),
            compiler_params=params,
        )(place, logit)
        bit = 1
        while bit < side * side:
            moves = [(i, i ^ bit) for i in range(side * side)]
            own = own + lax.ppermute(own, "ctx", moves)
            bit *= 2
        return own, spread

    own, spread = unit(over_ctx, (own, place, logit))
    combined = pl.pallas_call(
        lambda *refs: combine_kernel(cap, depth, *refs),
        out_shape=jax.ShapeDtypeStruct((tokens, width), jnp.bfloat16),
        out_specs=pl.BlockSpec(memory_space=pl.ANY),
        scratch_shapes=[
            pltpu.VMEM((QUARTERS, tokens, part), jnp.bfloat16),
            pltpu.SemaphoreType.DMA((QUARTERS,)),
        ],
        compiler_params=params,
    )(spread, router_weight, copies)
    return combined[None], own[0]


def solution(mesh):
    in_specs = (
        P("exp", "ctx", None),
        P("exp", "ctx", None),
        P("exp", "ctx", None),
        P(),
        P("ctx", "exp", None, None),
        P("ctx", "exp", None),
    )
    out_specs = (P("exp", "ctx", None), P("exp", None))
    side = round(mesh.shape["ctx"] ** 0.5)

    def step(*arrays):
        return shards(side, *arrays)

    return jax.shard_map(step, mesh=mesh, in_specs=in_specs, out_specs=out_specs, check_vma=False)
```
